512 devices in a mesh: uly: 16 (over y, x), fsdp: 8 (over z_lo, core), rep: 4 (over z_hi).
Axes of the slice: x: 4, y: 4, z: 16 (z_hi: 4, z_lo: 4; z = z_hi * 4 + z_lo), core: 2. Of those that a mesh axis runs over, the one named last changes fastest.
Arguments:
- inputs_norm: bfloat16 [64, 1024, 8192], P(('rep', 'fsdp'), 'uly'), parts along dimension 0, may hold values from -17 to 17
- queries: bfloat16 [64, 1024, 4096], P(('rep', 'fsdp'), 'uly'), parts along dimension 0, may hold values from -8 to 8
- key_states: bfloat16 [64, 1024, 512], P(('rep', 'fsdp'), 'uly'), parts along dimension 0, may hold values from -8 to 8
- value_states: bfloat16 [64, 1024, 512], P(('rep', 'fsdp'), 'uly'), parts along dimension 0, may hold values from -4.5 to 4.5
- context_grad: bfloat16 [64, 1024, 4096], P(('rep', 'fsdp'), 'uly'), parts along dimension 0, may hold values from -17 to 17
Outputs:
- key_weight_grad: bfloat16 [32768, 512], P(('rep', 'uly', 'fsdp')), parts along dimension 0
The draws below stay inside these ranges and needn't reach their ends.
There are 4 independent parts, one for each index of `rep`. The reference program is written for one: setup_inputs(seed, part) draws one part's arguments, and reference() takes and returns one part's arrays. A program takes and returns all parts, laid end to end along the dimension named above; each array names one. Nothing has to cross between parts.
All inputs are finite; a program needn't handle non-finite values. Where the reference program divides by a largest or mean magnitude, that divisor is 1e-20 or more.
Results may differ from the reference program's by a relative error of at most 0.029.
Values may be sent and summed in bfloat16 or wider, within the bound.
A program may use at most 128 MiB of HBM per device.

```python
import math
import jax
import jax.numpy as jnp
from jax import lax

D = 8192
QH = 32
KVH = 4
HD = 128
S = 1024
SEQS = 16
N_ULY = 16


def rising_scale():
    seq_frac = jnp.arange(SEQS, dtype=jnp.float32)[:, None] / SEQS
    tok_frac = jnp.arange(S, dtype=jnp.float32)[None, :] / S
    return jnp.exp(math.log(3.0) * (0.3 * seq_frac + 0.7 * tok_frac))


def event_signs(key):
    flips = jax.random.randint(key, (SEQS, 4, HD), 0, 2)
    return (2 * flips - 1).astype(jnp.float32)


def rising_field(key, width):
    base_key = jax.random.fold_in(key, 0)
    scale = rising_scale()[:, :, None]
    shape = (SEQS, S, width)
    base = jnp.clip(jax.random.normal(base_key, shape, jnp.float32), -4.0, 4.0)
    return (base * scale).astype(jnp.bfloat16)


def draw_inputs_norm(key, part):
    key = jax.random.fold_in(key, 11)
    return rising_field(key, D)


def draw_context_grad(key, part):
    key = jax.random.fold_in(key, 12)
    return rising_field(key, QH * HD)


def base_field(key, shape):
    return jnp.clip(jax.random.normal(key, shape, jnp.float32), -4.5, 4.5)


def draw_queries(key, part):
    signs = event_signs(key)
    key = jax.random.fold_in(key, 13)
    base = base_field(key, (SEQS, S, QH * HD))
    group_size = QH // KVH
    for event_index in range(4):
        strength = (5.0, 6.5, 8.0, 8.0)[event_index]
        head_index = event_index % KVH * group_size + event_index % group_size
        base = base.at[:, S - 1 - event_index, head_index * HD:(head_index + 1) * HD].set(strength * signs[:, event_index, :])
    return base.astype(jnp.bfloat16)


def draw_key_states(key, part):
    signs = event_signs(key)
    key = jax.random.fold_in(key, 14)
    base = base_field(key, (SEQS, S, KVH * HD))
    for event_index in range(4):
        strength = (5.0, 6.5, 8.0, 8.0)[event_index]
        head_index = event_index % KVH
        aligned = strength * signs[:, event_index, :]
        shrink = 1.0 - 2.0 * math.sqrt(HD) / (HD * strength * strength)
        base = base.at[:, 3 * event_index, head_index * HD:(head_index + 1) * HD].set(aligned)
        base = base.at[:, 3 * event_index + 1, head_index * HD:(head_index + 1) * HD].set(aligned * shrink)
    return base.astype(jnp.bfloat16)


def levels(stream_key, extent, pieces, low, largest):
    level, own = 1.0, jax.random.fold_in(stream_key, 6)
    for dim, blocks in pieces:
        heights = jnp.exp(jax.random.uniform(jax.random.fold_in(own, dim), (blocks,), jnp.float32, low / len(pieces), largest / len(pieces)))
        level = level * jnp.repeat(heights, extent[dim] // blocks).reshape([-1 if axis == dim else 1 for axis in range(len(extent))])
    return level


def noise(stream_key, shape, deviation, reach, cuts=(), kind=jnp.bfloat16):
    result = deviation * jax.random.normal(stream_key, shape, jnp.float32)
    if cuts:
        result = result * levels(stream_key, shape, cuts, -0.22, 0.18)
    return jnp.clip(result, -reach, reach).astype(kind)


def setup_inputs(seed: int = 0, part: int = 0) -> dict:
    key_list = jax.random.split(jax.random.key(seed), 6)
    part_keys = jax.random.split(jax.random.fold_in(key_list[5], part), 6)
    return {
        "inputs_norm": draw_inputs_norm(jax.random.fold_in(jax.random.fold_in(key_list[5], part), 71), part),
        "queries": draw_queries(jax.random.fold_in(jax.random.fold_in(key_list[5], part), 71), part),
        "key_states": draw_key_states(jax.random.fold_in(jax.random.fold_in(key_list[5], part), 71), part),
        "value_states": noise(part_keys[3], (SEQS, S, KVH * HD), 1.0, 4.5, ((0, 8), (1, 16))),
        "context_grad": draw_context_grad(jax.random.fold_in(jax.random.fold_in(key_list[5], part), 71), part),
    }


def head_key_grad(operands):
    query_head, key_head, value_head, grad_head = operands
    score_scale = 1.0 / math.sqrt(HD)
    positions = jnp.arange(S)
    visible = positions[:, None] >= positions[None, :]
    scores = jnp.dot(query_head, key_head.T, preferred_element_type=jnp.float32) * score_scale
    scores = jnp.where(visible, scores, -jnp.inf)
    top_score = lax.optimization_barrier(jnp.max(scores, axis=-1, keepdims=True))
    attn_probs = jnp.exp(scores - top_score)
    attn_probs = attn_probs / lax.optimization_barrier(jnp.sum(attn_probs, axis=-1, keepdims=True))
    prob_grad = jnp.dot(grad_head, value_head.T, preferred_element_type=jnp.float32)
    row_terms = lax.optimization_barrier(jnp.sum(attn_probs * prob_grad, axis=-1, keepdims=True))
    score_grad = (attn_probs * (prob_grad - row_terms) * score_scale).astype(jnp.bfloat16)
    return jnp.dot(score_grad.T, query_head, preferred_element_type=jnp.float32)

def sequence_key_grad(operands):
    queries, key_states, value_states, context_grad = operands
    group_size = QH // KVH
    query_heads = queries.reshape(S, QH, HD).transpose(1, 0, 2)
    grad_heads = context_grad.reshape(S, QH, HD).transpose(1, 0, 2)
    key_heads = jnp.repeat(key_states.reshape(S, KVH, HD).transpose(1, 0, 2), group_size, axis=0)
    value_heads = jnp.repeat(value_states.reshape(S, KVH, HD).transpose(1, 0, 2), group_size, axis=0)
    per_head = lax.map(head_key_grad, (query_heads, key_heads, value_heads, grad_heads))
    partial_grads = lax.optimization_barrier(jnp.sum(per_head.reshape(N_ULY, QH // N_ULY, S, HD), axis=1)).astype(jnp.bfloat16)
    summed = lax.optimization_barrier(jnp.sum(partial_grads.astype(jnp.float32).reshape(KVH, N_ULY // KVH, S, HD), axis=1))
    summed = summed.astype(jnp.bfloat16)
    return summed.transpose(1, 0, 2).reshape(S, KVH * HD)

def reference(inputs_norm, queries, key_states, value_states, context_grad):
    key_grad = lax.map(sequence_key_grad, (queries, key_states, value_states, context_grad))
    input_max = jnp.max(jnp.abs(inputs_norm.astype(jnp.float32)))
    key_max = jnp.max(jnp.abs(key_grad.astype(jnp.float32)))
    raw_grad = jnp.dot(inputs_norm.reshape(-1, D).T, key_grad.reshape(-1, KVH * HD), preferred_element_type=jnp.float32)
    factor = 36.0 / (input_max * key_max) / math.sqrt(S * SEQS)
    return (raw_grad * factor).astype(jnp.bfloat16)
```

```python
import math

import jax
import jax.numpy as jnp
from jax import lax
from jax.experimental import pallas as pl
from jax.experimental.pallas import tpu as pltpu
from jax.sharding import PartitionSpec as P

MESH = pl.DeviceIdType.MESH
KVH = 4
HD = 128
SIDE = 4
ULY = SIDE * SIDE
FSDP = 8
SEQ = 2
TOK = 64
GROUP = 8
WIDTH = 8192
BAND = 1024
SLAB = BAND // SIDE
OUT_ROWS = 64
COLS = KVH * HD
SCALE = 1.0 / math.sqrt(HD)
LOG2E = math.log2(math.e)


def kernel(
    x_hbm, q_hbm, k_hbm, v_hbm, g_hbm, out_ref,
    qg, gg, kg, vg, xr, xt, dkacc, part, part_in, dkf, dka, acc,
    y_out, y_in, z_out, z_in, m_own, m_row, m_y_out, m_y_in, m_z_out, m_z_in,
    q_recv, g_recv, kv_recv, x_recv, part_recv, dk_recv, fwd_recv, y_recv, z_recv, m_recv,
    q_send, g_send, kv_send, x_send, part_send, dk_send, fwd_send, y_send, z_send, m_send,
):
    u = lax.axis_index("uly")
    f = lax.axis_index("fsdp")
    y, x = lax.div(u, SIDE), lax.rem(u, SIDE)
    z, c = lax.div(f, 2), lax.rem(f, 2)
    other = 2 * z + 1 - c
    home = lax.div(f, SIDE)

    def to(du, df):
        return {"uly": du, "fsdp": df}

    def remote(src, dst, send, recv, device):
        return pltpu.make_async_remote_copy(
            src_ref=src, dst_ref=dst, send_sem=send, recv_sem=recv,
            device_id=device, device_id_type=MESH,
        )

    def drain(ref, sem):
        pltpu.make_async_copy(ref, ref, sem).wait()

    def ring(offset):
        return lax.rem(u + offset, ULY)

    def row_mate(offset):
        return SIDE * y + lax.rem(x + offset, SIDE)

    def column_mate(offset):
        return SIDE * lax.rem(y + offset, SIDE) + x

    barrier = pltpu.get_barrier_semaphore()

    def greet(device):
        pl.semaphore_signal(barrier, inc=1, device_id=device, device_id_type=MESH)

    for d in range(1, ULY):
        greet(to(ring(d), f))
    for d in range(SIDE):
        greet(to(row_mate(d), other))
    for source_z in range(SIDE):
        source = 2 * source_z + home
        pl.when(source != f)(lambda source=source: greet(to(u, source)))

    for s in range(SEQ):
        cols = pl.ds(pl.multiple_of(y * GROUP * HD, GROUP * HD), GROUP * HD)
        pltpu.make_async_copy(q_hbm.at[s, :, cols], qg.at[s, y], q_recv.at[s]).start()
        pltpu.make_async_copy(g_hbm.at[s, :, cols], gg.at[s, y], g_recv.at[s]).start()
    own_cols = pl.ds(pl.multiple_of(y * HD, HD), HD)
    pltpu.make_async_copy(k_hbm.at[:, :, own_cols], kg.at[:, u], kv_recv.at[0]).start()
    pltpu.make_async_copy(v_hbm.at[:, :, own_cols], vg.at[:, u], kv_recv.at[1]).start()

    def feature_cols(slab, target_x, half):
        start = (slab * SIDE + target_x) * (2 * SLAB) + half * SLAB
        return pl.ds(pl.multiple_of(start, SLAB), SLAB)

    for slab in range(SIDE):
        pltpu.make_async_copy(
            x_hbm.at[:, :, feature_cols(slab, x, c)],
            xr.at[:, 0, x, :, pl.ds(slab * SLAB, SLAB)],
            x_recv,
        ).start()

    pl.semaphore_wait(barrier, ULY - 1 + SIDE + SIDE - jnp.where(home == c, 1, 0))

    def send_heads(s):
        for d in range(1, SIDE):
            target_y = lax.rem(y + d, SIDE)
            cols = pl.ds(pl.multiple_of(target_y * GROUP * HD, GROUP * HD), GROUP * HD)
            device = to(column_mate(d), f)
            remote(q_hbm.at[s, :, cols], qg.at[s, y], q_send.at[s], q_recv.at[s], device).start()
            remote(g_hbm.at[s, :, cols], gg.at[s, y], g_send.at[s], g_recv.at[s], device).start()

    for d in range(1, ULY):
        target = ring(d)
        cols = pl.ds(pl.multiple_of(lax.div(target, SIDE) * HD, HD), HD)
        device = to(target, f)
        remote(k_hbm.at[:, :, cols], kg.at[:, u], kv_send.at[0], kv_recv.at[0], device).start()
        remote(v_hbm.at[:, :, cols], vg.at[:, u], kv_send.at[1], kv_recv.at[1], device).start()
    send_heads(0)
    send_heads(1)
    for dc in range(2):
        for d in range(SIDE):
            if dc == 0 and d == 0:
                continue
            target_x = lax.rem(x + d, SIDE)
            half = c if dc == 0 else 1 - c
            for slab in range(SIDE):
                remote(
                    x_hbm.at[:, :, feature_cols(slab, target_x, half)],
                    xr.at[:, dc, x, :, pl.ds(slab * SLAB, SLAB)],
                    x_send.at[dc], x_recv,
                    to(row_mate(d), f if dc == 0 else other),
                ).start()

    rows = GROUP * TOK
    chunk = SIDE * TOK
    key_at = lax.broadcasted_iota(jnp.int32, (chunk, rows), 0)
    query_at = lax.rem(lax.broadcasted_iota(jnp.int32, (chunk, rows), 1), TOK) + x * TOK
    hidden = key_at > query_at

    def heads_to_rows(block):
        return jnp.concatenate([block[:, h * HD:(h + 1) * HD] for h in range(GROUP)], axis=0)

    def nt(a, b):
        return lax.dot_general(a, b, (((1,), (1,)), ((), ())), preferred_element_type=jnp.float32)

    def attend(s):
        for j in range(SIDE):
            query = heads_to_rows(qg[s, j])
            grad = heads_to_rows(gg[s, j])
            scores = []
            for n in range(j + 1):
                keys = kg[s, SIDE * n:SIDE * (n + 1)].reshape(chunk, HD)
                scores.append(nt(keys, query) * (SCALE * LOG2E))
            scores[j] = jnp.where(hidden, -jnp.inf, scores[j])
            top = jnp.max(scores[0], axis=0, keepdims=True)
            for n in range(1, j + 1):
                top = jnp.maximum(top, jnp.max(scores[n], axis=0, keepdims=True))
            exps = [jnp.exp2(block - top) for block in scores]
            prob_grads = []
            for n in range(j + 1):
                values = vg[s, SIDE * n:SIDE * (n + 1)].reshape(chunk, HD)
                prob_grads.append(nt(values, grad))
            total = sum(jnp.sum(e, axis=0, keepdims=True) for e in exps)
            weighted = sum(
                jnp.sum(e * p, axis=0, keepdims=True) for e, p in zip(exps, prob_grads)
            )
            row_terms = weighted / total
            scale = SCALE / total
            for n in range(j + 1):
                score_grad = (exps[n] * ((prob_grads[n] - row_terms) * scale)).astype(jnp.bfloat16)
                term = jnp.dot(score_grad, query, preferred_element_type=jnp.float32)
                term = term.reshape(SIDE, TOK, HD)
                if n == j:
                    dkacc[s, n] = term
                else:
                    dkacc[s, n] += term

    def send_partials(s):
        for target_x in range(SIDE):
            part[s, target_x] = dkacc[s, :, target_x].astype(jnp.bfloat16)
        for d in range(1, SIDE):
            remote(
                part.at[s, lax.rem(x + d, SIDE)], part_in.at[s, d - 1],
                part_send.at[s], part_recv.at[s], to(row_mate(d), f),
            ).start()

    def send_key_grad(s):
        drain(part_in.at[s], part_recv.at[s])
        summed = dkacc[s, :, x]
        for d in range(SIDE - 1):
            summed += part_in[s, d].astype(jnp.float32)
        dkf[s] = summed.astype(jnp.bfloat16)
        for d in range(1, ULY):
            target = ring(d)
            remote(
                dkf.at[s, lax.div(target, SIDE)],
                dka.at[s, 0, x, :, own_cols],
                dk_send.at[s], dk_recv.at[s], to(target, f),
            ).start()
        pltpu.make_async_copy(
            dkf.at[s, y], dka.at[s, 0, x, :, own_cols], dk_recv.at[s]
        ).start()
        return jnp.max(jnp.abs(summed))

    def forward(s):
        drain(dka.at[s, 0], dk_recv.at[s])
        remote(dka.at[s, 0], dka.at[s, 1], fwd_send.at[s], fwd_recv.at[s], to(u, other)).start()

    def grad_rows(s):
        return dka[s].reshape(2 * SIDE * TOK, COLS)

    for s in range(SEQ):
        drain(qg.at[s], q_recv.at[s])
        drain(gg.at[s], g_recv.at[s])
        if s == 0:
            drain(kg, kv_recv.at[0])
            drain(vg, kv_recv.at[1])
        attend(s)
        send_partials(s)
        if s == 0:
            key_max = send_key_grad(0)

    drain(xr, x_recv)
    input_max = jnp.float32(0.0)
    for s in range(SEQ):
        block = xr[s].reshape(2 * SIDE * TOK, BAND)
        tops = jnp.max(jnp.abs(block), axis=0, keepdims=True).astype(jnp.float32)
        input_max = jnp.maximum(input_max, jnp.max(tops))
        xt[s] = block.T
    forward(0)
    key_max = jnp.maximum(key_max, send_key_grad(1))
    row_at = lax.broadcasted_iota(jnp.int32, (8, HD), 0)
    m_own[...] = jnp.where(row_at < 4, input_max, key_max)
    for dc in range(2):
        for d in range(SIDE):
            if dc or d:
                remote(
                    m_own, m_row.at[dc * SIDE + d - 1], m_send.at[0], m_recv.at[0],
                    to(row_mate(d), f if dc == 0 else other),
                ).start()
    drain(dka.at[0, 1], fwd_recv.at[0])
    acc[...] = jnp.dot(xt[0], grad_rows(0), preferred_element_type=jnp.float32)
    forward(1)
    drain(m_row, m_recv.at[0])
    m_y_out[...] = jnp.maximum(m_own[...], jnp.max(m_row[...], axis=0))
    for d in range(1, SIDE):
        remote(
            m_y_out, m_y_in.at[d - 1], m_send.at[1], m_recv.at[1], to(column_mate(d), f)
        ).start()
    drain(dka.at[1, 1], fwd_recv.at[1])

    def slab_grad(target_y):
        at = pl.ds(pl.multiple_of(target_y * SLAB, SLAB), SLAB)
        return acc[at] + jnp.dot(xt[1, at], grad_rows(1), preferred_element_type=jnp.float32)

    for d in range(1, SIDE):
        y_out[d - 1] = slab_grad(lax.rem(y + d, SIDE)).astype(jnp.bfloat16)
        remote(
            y_out.at[d - 1], y_in.at[d - 1], y_send.at[d - 1], y_recv.at[d - 1],
            to(column_mate(d), f),
        ).start()
    slab_sum = slab_grad(y)
    drain(m_y_in, m_recv.at[1])
    m_z_out[...] = jnp.maximum(m_y_out[...], jnp.max(m_y_in[...], axis=0))
    for d in range(1, SIDE):
        drain(y_in.at[d - 1], y_recv.at[d - 1])
        slab_sum += y_in[d - 1].astype(jnp.float32)
    z_out[...] = slab_sum.reshape(SIDE, OUT_ROWS, COLS).astype(jnp.bfloat16)
    for k in range(SIDE):
        target = SIDE * c + k

        def away(k=k, target=target):
            remote(z_out.at[k], z_in.at[z], z_send.at[0], z_recv, to(u, target)).start()
            remote(m_z_out, m_z_in.at[z], m_send.at[2], m_recv.at[2], to(u, target)).start()

        def stay(k=k):
            pltpu.make_async_copy(z_out.at[k], z_in.at[z], z_recv).start()
            pltpu.make_async_copy(m_z_out, m_z_in.at[z], m_recv.at[2]).start()

        pl.when(target != f)(away)
        pl.when(target == f)(stay)
    drain(m_z_in, m_recv.at[2])
    drain(z_in, z_recv)
    largest = jnp.max(m_z_in[...], axis=0)
    input_top = jnp.max(largest[0:4], axis=0, keepdims=True)[:, 0:1]
    key_top = jnp.max(largest[4:8], axis=0, keepdims=True)[:, 0:1]
    factor = 36.0 / (input_top * key_top) / math.sqrt(SEQ * FSDP * ULY * TOK)
    raw = z_in[0].astype(jnp.float32)
    for source_z in range(1, SIDE):
        raw += z_in[source_z].astype(jnp.float32)
    out_ref[...] = (raw * factor).astype(jnp.bfloat16)

    for s in range(SEQ):
        drain(qg.at[s, 0:SIDE - 1], q_send.at[s])
        drain(gg.at[s, 0:SIDE - 1], g_send.at[s])
        drain(part_in.at[s], part_send.at[s])
        drain(kg.at[s, 0:ULY - 1], dk_send.at[s])
        drain(dka.at[s, 0], fwd_send.at[s])
    drain(kg.at[:, 0:ULY - 1], kv_send.at[0])
    drain(vg.at[:, 0:ULY - 1], kv_send.at[1])
    drain(xr.at[:, 0, 0:SIDE - 1], x_send.at[0])
    drain(xr.at[:, 1], x_send.at[1])
    for d in range(1, SIDE):
        drain(y_out.at[d - 1], y_send.at[d - 1])
    drain(m_row, m_send.at[0])
    drain(m_y_in, m_send.at[1])

    def drain_last(count):
        drain(z_in.at[0:count], z_send.at[0])
        drain(m_z_in.at[0:count], m_send.at[2])

    pl.when(home == c)(lambda: drain_last(SIDE - 1))
    pl.when(home != c)(lambda: drain_last(SIDE))


def per_device(inputs_norm, queries, key_states, value_states, context_grad):
    bf16, f32 = jnp.bfloat16, jnp.float32
    vmem, dma = pltpu.VMEM, pltpu.SemaphoreType.DMA
    return pl.pallas_call(
        kernel,
        out_shape=jax.ShapeDtypeStruct((OUT_ROWS, COLS), bf16),
        in_specs=[pl.BlockSpec(memory_space=pl.ANY)] * 5,
        out_specs=pl.BlockSpec(memory_space=pltpu.VMEM),
        scratch_shapes=[
            vmem((SEQ, SIDE, TOK, GROUP * HD), bf16),
            vmem((SEQ, SIDE, TOK, GROUP * HD), bf16),
            vmem((SEQ, ULY, TOK, HD), bf16),
            vmem((SEQ, ULY, TOK, HD), bf16),
            vmem((SEQ, 2, SIDE, TOK, BAND), bf16),
            vmem((SEQ, BAND, 2 * SIDE * TOK), bf16),
            vmem((SEQ, SIDE, SIDE, TOK, HD), f32),
            vmem((SEQ, SIDE, SIDE, TOK, HD), bf16),
            vmem((SEQ, SIDE - 1, SIDE, TOK, HD), bf16),
            vmem((SEQ, SIDE, TOK, HD), bf16),
            vmem((SEQ, 2, SIDE, TOK, COLS), bf16),
            vmem((BAND, COLS), f32),
            vmem((SIDE - 1, SLAB, COLS), bf16),
            vmem((SIDE - 1, SLAB, COLS), bf16),
            vmem((SIDE, OUT_ROWS, COLS), bf16),
            vmem((SIDE, OUT_ROWS, COLS), bf16),
            vmem((8, HD), f32),
            vmem((2 * SIDE - 1, 8, HD), f32),
            vmem((8, HD), f32),
            vmem((SIDE - 1, 8, HD), f32),
            vmem((8, HD), f32),
            vmem((SIDE, 8, HD), f32),
            dma((SEQ,)), dma((SEQ,)), dma((2,)), dma, dma((SEQ,)),
            dma((SEQ,)), dma((SEQ,)), dma((SIDE - 1,)), dma, dma((3,)),
            dma((SEQ,)), dma((SEQ,)), dma((2,)), dma((2,)), dma((SEQ,)),
            dma((SEQ,)), dma((SEQ,)), dma((SIDE - 1,)), dma((1,)), dma((3,)),
        ],
        compiler_params=pltpu.CompilerParams(
            collective_id=0, has_side_effects=True, vmem_limit_bytes=56 * 1024 * 1024
        ),
    )(inputs_norm, queries, key_states, value_states, context_grad)


def solution(mesh):
    placed = P(("rep", "fsdp"), "uly", None)
    return jax.shard_map(
        per_device,
        mesh=mesh,
        in_specs=(placed,) * 5,
        out_specs=P(("rep", "uly", "fsdp"), None),
        check_vma=False,
    )
```

```python
import functools
import math

import jax
import jax.numpy as jnp
from jax import lax
from jax.experimental import pallas as pl
from jax.experimental.pallas import tpu as pltpu
from jax.sharding import PartitionSpec as P

MESH = pl.DeviceIdType.MESH
KVH = 4
HD = 128
SIDE = 4
ULY = SIDE * SIDE
FSDP = 8
SEQ = 2
TOK = 64
GROUP = 8
WIDTH = 8192
BAND = 1024
SLAB = BAND // SIDE
OUT_ROWS = 64
COLS = KVH * HD
PART = 256
SCALE = 1.0 / math.sqrt(HD)
LOG2E = math.log2(math.e)


def kernel(
    x_hbm, q_hbm, k_hbm, v_hbm, g_hbm, out_ref,
    qg, kv, xr, xt, dkacc, part, part_in, dkf, dka, acc,
    y_out, y_in, z_out, z_in, top, m_own, m_row, m_y_out, m_y_in, m_z_out, m_z_in,
    q_recv, kv_recv, kv_all_recv, x_recv, part_recv, dk_recv, y_recv, z_recv, m_recv,
    q_send, kv_send, kv_all_send, x_send, part_send, dk_send, y_send, z_send, m_send,
):
    u = lax.axis_index("uly")
    f = lax.axis_index("fsdp")
    y, x = lax.div(u, SIDE), lax.rem(u, SIDE)
    z, c = lax.div(f, 2), lax.rem(f, 2)
    other = 2 * z + 1 - c
    home = lax.div(f, SIDE)

    def to(du, df):
        return {"uly": du, "fsdp": df}

    def remote(src, dst, send, recv, device):
        return pltpu.make_async_remote_copy(
            src_ref=src, dst_ref=dst, send_sem=send, recv_sem=recv,
            device_id=device, device_id_type=MESH,
        )

    def drain(ref, sem):
        pltpu.make_async_copy(ref, ref, sem).wait()

    def span(start, size):
        return pl.ds(pl.multiple_of(start, size), size)

    def ring(offset):
        return lax.rem(u + offset, ULY)

    place = (x, y)

    def along(axis, offset):
        return lax.rem(place[axis] + offset, SIDE)

    def mate(axis, offset):
        return SIDE * y + along(0, offset) if axis == 0 else SIDE * along(1, offset) + x

    def pick(half, for_first, for_second):
        return jnp.where(half == 0, for_first, for_second)

    barrier = pltpu.get_barrier_semaphore()

    def greet(device):
        pl.semaphore_signal(barrier, inc=1, device_id=device, device_id_type=MESH)

    for d in range(1, ULY):
        greet(to(ring(d), f))
    for d in range(ULY):
        greet(to(ring(d), other))
    for source_z in range(SIDE):
        source = 2 * source_z + home
        pl.when(source != f)(lambda source=source: greet(to(u, source)))

    def kv_here(s):
        return kv.at[:, 0, y] if s == 0 else kv.at[:, 1, :, x]

    def send_heads(s, d):
        target = along(s, d)
        cols = span(target * GROUP * HD, GROUP * HD)
        for which, hbm in enumerate((q_hbm, g_hbm)):
            src, dst = hbm.at[s, :, cols], qg.at[s, place[s], which]
            if d == 0:
                pltpu.make_async_copy(src, dst, q_recv.at[s, d]).start()
            else:
                remote(src, dst, q_send.at[s], q_recv.at[s, d], to(mate(s, d), f)).start()

    def send_kv(s, d):
        cols = span(along(s, d) * HD, HD)
        for which, hbm in enumerate((k_hbm, v_hbm)):
            src, dst = hbm.at[s, :, cols], kv.at[which, s, y, x]
            if d == 0:
                pltpu.make_async_copy(src, dst, kv_recv.at[s]).start()
            else:
                remote(src, dst, kv_send.at[s], kv_recv.at[s], to(mate(s, d), f)).start()

    def send_inputs(same, d):
        half = c if same else 1 - c
        own = pick(half, x, y)
        target = lax.rem(own + d, SIDE)
        device = to(pick(half, mate(0, d), mate(1, d)), 2 * z + half)
        for slab in range(SIDE):
            start = pick(half, (slab * SIDE + target) * 2, (target * SIDE + slab) * 2 + 1)
            src = x_hbm.at[:, :, span(start * SLAB, SLAB)]
            dst = xr.at[:, 0 if same else 1, own, :, pl.ds(slab * SLAB, SLAB)]
            if same and d == 0:
                pltpu.make_async_copy(src, dst, x_recv).start()
            else:
                remote(src, dst, x_send.at[0 if same else 1], x_recv, device).start()

    for s in range(SEQ):
        send_kv(s, 0)
    for s in range(SEQ):
        send_heads(s, 0)
    send_inputs(True, 0)
    pl.semaphore_wait(barrier, 2 * ULY - 1 + SIDE - jnp.where(home == c, 1, 0))
    for s in range(SEQ):
        for d in range(1, SIDE):
            send_kv(s, d)
    for d in range(1, SIDE):
        for s in range(SEQ):
            send_heads(s, d)
    dkacc[...] = jnp.zeros_like(dkacc)
    for s in range(SEQ):
        drain(kv_here(s), kv_recv.at[s])
        for d in range(1, SIDE):
            remote(
                kv_here(s), kv_here(s), kv_all_send.at[s], kv_all_recv.at[s],
                to(mate(1 - s, d), f),
            ).start()
    for d in range(SIDE):
        if d:
            send_inputs(True, d)
        send_inputs(False, d)

    rows = GROUP * TOK
    chunk = SIDE * TOK

    def heads_to_rows(block):
        return jnp.concatenate([block[:, h * HD:(h + 1) * HD] for h in range(GROUP)], axis=0)

    def nt(a, b):
        return lax.dot_general(a, b, (((1,), (1,)), ((), ())), preferred_element_type=jnp.float32)

    def attend_to(s, slot, chunks, block_x):
        query = heads_to_rows(qg[s, slot, 0])
        grad = heads_to_rows(qg[s, slot, 1])
        key_at = lax.broadcasted_iota(jnp.int32, (chunk, rows), 0)
        query_at = lax.rem(lax.broadcasted_iota(jnp.int32, (chunk, rows), 1), TOK)
        scores = []
        for n in range(chunks):
            keys = kv[0, s, n].reshape(chunk, HD)
            scores.append(nt(keys, query) * (SCALE * LOG2E))
        scores[-1] = jnp.where(key_at > query_at + block_x * TOK, -jnp.inf, scores[-1])
        top_score = jnp.max(scores[0], axis=0, keepdims=True)
        for block in scores[1:]:
            top_score = jnp.maximum(top_score, jnp.max(block, axis=0, keepdims=True))
        exps = [jnp.exp2(block - top_score) for block in scores]
        prob_grads = []
        for n in range(chunks):
            values = kv[1, s, n].reshape(chunk, HD)
            prob_grads.append(nt(values, grad))
        total = sum(jnp.sum(e, axis=0, keepdims=True) for e in exps)
        weighted = sum(jnp.sum(e * p, axis=0, keepdims=True) for e, p in zip(exps, prob_grads))
        row_terms = weighted / total
        scale = SCALE / total
        for n in range(chunks):
            score_grad = (exps[n] * ((prob_grads[n] - row_terms) * scale)).astype(jnp.bfloat16)
            term = jnp.dot(score_grad, query, preferred_element_type=jnp.float32)
            dkacc[s, n] += term.reshape(SIDE, TOK, HD)

    def attend(s, d):
        slot = lax.rem(place[s] - d + SIDE, SIDE)
        drain(qg.at[s, slot], q_recv.at[s, d])
        block_y, block_x = (y, slot) if s == 0 else (slot, x)
        for chunks in range(1, SIDE + 1):
            pl.when(block_y == chunks - 1)(
                functools.partial(attend_to, s, slot, chunks, block_x)
            )

    def keys_of(s, index):
        return dkacc[0, index] if s == 0 else dkacc[1, :, index]

    def send_partials(s):
        for index in range(SIDE):
            part[s, index] = keys_of(s, index).astype(jnp.bfloat16)
        for d in range(1, SIDE):
            remote(
                part.at[s, along(1 - s, d)], part_in.at[s, d - 1],
                part_send.at[s], part_recv.at[s], to(mate(1 - s, d), f),
            ).start()

    def send_key_grad(s):
        drain(part_in.at[s], part_recv.at[s])
        summed = keys_of(s, place[1 - s])
        for d in range(SIDE - 1):
            summed += part_in[s, d].astype(jnp.float32)
        dkf[s] = summed.astype(jnp.bfloat16)
        largest = jnp.max(jnp.abs(summed).reshape(SIDE * TOK // 8, 8, HD), axis=0)
        top[...] = largest if s == 0 else jnp.maximum(top[...], largest)
        cols = span(place[s] * HD, HD)

        def copy(half, src, slot, device, here, send):
            dst = dka.at[s, jnp.where(c == half, 0, 1), slot, :, cols]

            def away():
                remote(src, dst, send, dk_recv.at[s], device).start()

            def stay():
                pltpu.make_async_copy(src, dst, dk_recv.at[s]).start()

            if here:
                pl.when(c == half)(stay)
                pl.when(c != half)(away)
            else:
                away()

        for d in range(ULY):
            block = (lax.rem if s == 0 else lax.div)(ring(d), SIDE)
            copy(
                1 - s, dkf.at[s, block], place[1 - s], to(ring(d), 2 * z + 1 - s),
                d == 0, dk_send.at[s, 1],
            )
        for d in range(SIDE):
            copy(
                s, dkf.at[s], slice(None), to(mate(s, d), 2 * z + s), d == 0, dk_send.at[s, 0]
            )

    def grad_rows(s, cols):
        return dka[s, :, :, :, cols].reshape(2 * SIDE * TOK, -1)

    for s in range(SEQ):
        drain(kv.at[:, 0, 0:SIDE - 1] if s == 0 else kv.at[:, 1, :, 0:SIDE - 1], kv_all_recv.at[s])

        def step(d, carry, s=s):
            if s == 1:
                pl.when(d == SIDE - 1)(lambda: send_key_grad(0))
            attend(s, d)
            return carry

        lax.fori_loop(0, SIDE, step, 0)
        send_partials(s)
    send_key_grad(1)

    drain(xr, x_recv)
    input_max = jnp.float32(0.0)
    for s in range(SEQ):
        block = xr[s].reshape(2 * SIDE * TOK, BAND)
        tops = jnp.max(jnp.abs(block), axis=0, keepdims=True).astype(jnp.float32)
        input_max = jnp.maximum(input_max, jnp.max(tops))
        xt[s] = block.T
    key_max = jnp.max(top[...])
    row_at = lax.broadcasted_iota(jnp.int32, (8, HD), 0)
    m_own[...] = jnp.where(row_at < 4, input_max, key_max)
    for dc in range(2):
        for d in range(SIDE):
            if dc or d:
                remote(
                    m_own, m_row.at[dc * SIDE + d - 1], m_send.at[0], m_recv.at[0],
                    to(mate(0, d), f if dc == 0 else other),
                ).start()
    drain(dka.at[0], dk_recv.at[0])
    acc[...] = jnp.dot(xt[0], grad_rows(0, slice(None)), preferred_element_type=jnp.float32)
    drain(m_row, m_recv.at[0])
    m_y_out[...] = jnp.maximum(m_own[...], jnp.max(m_row[...], axis=0))
    for d in range(1, SIDE):
        remote(
            m_y_out, m_y_in.at[d - 1], m_send.at[1], m_recv.at[1], to(mate(1, d), f)
        ).start()
    drain(dka.at[1], dk_recv.at[1])

    own = pick(c, y, x)

    def slab_grad(target, cols):
        at = span(target * SLAB, SLAB)
        return acc[at, cols] + jnp.dot(
            xt[1, at], grad_rows(1, cols), preferred_element_type=jnp.float32
        )

    parts = [slice(p * PART, (p + 1) * PART) for p in range(COLS // PART)]
    for p, cols in enumerate(parts):
        for d in range(1, SIDE):
            y_out[p, d - 1] = slab_grad(lax.rem(own + d, SIDE), cols).astype(jnp.bfloat16)
            remote(
                y_out.at[p, d - 1], y_in.at[p, d - 1], y_send.at[p], y_recv.at[p],
                to(pick(c, mate(1, d), mate(0, d)), f),
            ).start()
    sums = [slab_grad(own, cols) for cols in parts]
    drain(m_y_in, m_recv.at[1])
    m_z_out[...] = jnp.maximum(m_y_out[...], jnp.max(m_y_in[...], axis=0))

    def last_sends(k, src, dst, send, recv):
        target = SIDE * c + k

        def away():
            remote(src, dst, send, recv, to(u, target)).start()

        def stay():
            pltpu.make_async_copy(src, dst, recv).start()

        pl.when(target != f)(away)
        pl.when(target == f)(stay)

    for k in range(SIDE):
        last_sends(k, m_z_out, m_z_in.at[z], m_send.at[2], m_recv.at[2])
    for p in range(len(parts)):
        drain(y_in.at[p], y_recv.at[p])
        for d in range(SIDE - 1):
            sums[p] += y_in[p, d].astype(jnp.float32)
        z_out[p] = sums[p].reshape(SIDE, OUT_ROWS, PART).astype(jnp.bfloat16)
        for k in range(SIDE):
            last_sends(k, z_out.at[p, k], z_in.at[p, z], z_send.at[p], z_recv.at[p])
    drain(m_z_in, m_recv.at[2])
    largest = jnp.max(m_z_in[...], axis=0)
    input_top = jnp.max(largest[0:4], axis=0, keepdims=True)[:, 0:1]
    key_top = jnp.max(largest[4:8], axis=0, keepdims=True)[:, 0:1]
    factor = 36.0 / (input_top * key_top) / math.sqrt(SEQ * FSDP * ULY * TOK)
    for p, cols in enumerate(parts):
        drain(z_in.at[p], z_recv.at[p])
        raw = z_in[p, 0].astype(jnp.float32)
        for source_z in range(1, SIDE):
            raw += z_in[p, source_z].astype(jnp.float32)
        out_ref[:, cols] = (raw * factor).astype(jnp.bfloat16)

    for s in range(SEQ):
        drain(qg.at[s, 0:SIDE - 1], q_send.at[s])
        drain(kv.at[:, s, 0, 0:SIDE - 1], kv_send.at[s])
        drain(kv.at[:, s, 0:SIDE - 1], kv_all_send.at[s])
        drain(part_in.at[s], part_send.at[s])

        def drain_same(s=s):
            drain(part_in.at[s], dk_send.at[s, 0])
            drain(part.at[s], dk_send.at[s, 1])

        def drain_other(s=s):
            drain(part.at[s], dk_send.at[s, 0])
            drain(xt.at[s, 0:(ULY - 1) * TOK * HD // (2 * SIDE * TOK)], dk_send.at[s, 1])

        pl.when(c == s)(drain_same)
        pl.when(c != s)(drain_other)
    drain(xr.at[:, 0, 0:SIDE - 1], x_send.at[0])
    drain(xr.at[:, 1], x_send.at[1])
    for p in range(len(parts)):
        drain(y_in.at[p], y_send.at[p])
    drain(m_row, m_send.at[0])
    drain(m_y_in, m_send.at[1])

    def drain_last(count):
        for p in range(len(parts)):
            drain(z_in.at[p, 0:count], z_send.at[p])
        drain(m_z_in.at[0:count], m_send.at[2])

    pl.when(home == c)(lambda: drain_last(SIDE - 1))
    pl.when(home != c)(lambda: drain_last(SIDE))


def per_device(inputs_norm, queries, key_states, value_states, context_grad):
    bf16, f32 = jnp.bfloat16, jnp.float32
    parts = COLS // PART
    vmem, dma = pltpu.VMEM, pltpu.SemaphoreType.DMA
    return pl.pallas_call(
        kernel,
        out_shape=jax.ShapeDtypeStruct((OUT_ROWS, COLS), bf16),
        in_specs=[pl.BlockSpec(memory_space=pl.ANY)] * 5,
        out_specs=pl.BlockSpec(memory_space=pltpu.VMEM),
        scratch_shapes=[
            vmem((SEQ, SIDE, 2, TOK, GROUP * HD), bf16),
            vmem((2, SEQ, SIDE, SIDE, TOK, HD), bf16),
            vmem((SEQ, 2, SIDE, TOK, BAND), bf16),
            vmem((SEQ, BAND, 2 * SIDE * TOK), bf16),
            vmem((SEQ, SIDE, SIDE, TOK, HD), f32),
            vmem((SEQ, SIDE, SIDE, TOK, HD), bf16),
            vmem((SEQ, SIDE - 1, SIDE, TOK, HD), bf16),
            vmem((SEQ, SIDE, TOK, HD), bf16),
            vmem((SEQ, 2, SIDE, TOK, COLS), bf16),
            vmem((BAND, COLS), f32),
            vmem((parts, SIDE - 1, SLAB, PART), bf16),
            vmem((parts, SIDE - 1, SLAB, PART), bf16),
            vmem((parts, SIDE, OUT_ROWS, PART), bf16),
            vmem((parts, SIDE, OUT_ROWS, PART), bf16),
            vmem((8, HD), f32),
            vmem((8, HD), f32),
            vmem((2 * SIDE - 1, 8, HD), f32),
            vmem((8, HD), f32),
            vmem((SIDE - 1, 8, HD), f32),
            vmem((8, HD), f32),
            vmem((SIDE, 8, HD), f32),
            dma((SEQ, SIDE)), dma((SEQ,)), dma((SEQ,)), dma, dma((SEQ,)),
            dma((SEQ,)), dma((parts,)), dma((parts,)), dma((3,)),
            dma((SEQ,)), dma((SEQ,)), dma((SEQ,)), dma((2,)), dma((SEQ,)),
            dma((SEQ, 2)), dma((parts,)), dma((parts,)), dma((3,)),
        ],
        compiler_params=pltpu.CompilerParams(
            collective_id=0, has_side_effects=True, vmem_limit_bytes=56 * 1024 * 1024
        ),
    )(inputs_norm, queries, key_states, value_states, context_grad)


def solution(mesh):
    placed = P(("rep", "fsdp"), "uly", None)
    return jax.shard_map(
        per_device,
        mesh=mesh,
        in_specs=(placed,) * 5,
        out_specs=P(("rep", "uly", "fsdp"), None),
        check_vma=False,
    )
```

```python
import functools
import math

import jax
import jax.numpy as jnp
from jax import lax
from jax.experimental import pallas as pl
from jax.experimental.pallas import tpu as pltpu
from jax.sharding import PartitionSpec as P

MESH = pl.DeviceIdType.MESH
KVH = 4
HD = 128
SIDE = 4
ULY = SIDE * SIDE
FSDP = 8
SEQ = 2
TOK = 64
GROUP = 8
WIDTH = 8192
BAND = 1024
SLAB = BAND // SIDE
OUT_ROWS = 64
COLS = KVH * HD
INPUTS_AFTER = 0
GRAD_BEFORE = 0
PART = 128
SCALE = 1.0 / math.sqrt(HD)
LOG2E = math.log2(math.e)


def kernel(
    x_hbm, q_hbm, k_hbm, v_hbm, g_hbm, out_ref,
    qg, kv, xr, xt, dkacc, part, part_in, dkf, dka, acc,
    y_out, y_in, z_out, z_in, top, m_own, m_row, m_y_out, m_y_in, m_z_out, m_z_in,
    q_recv, kv_recv, kv_all_recv, x_recv, part_recv, chunk_recv, dk_recv, y_recv, z_recv, m_recv,
    q_send, kv_send, kv_all_send, x_send, part_send, chunk_send, dk_send, y_send, z_send, m_send,
):
    u = lax.axis_index("uly")
    f = lax.axis_index("fsdp")
    y, x = lax.div(u, SIDE), lax.rem(u, SIDE)
    z, c = lax.div(f, 2), lax.rem(f, 2)
    other = 2 * z + 1 - c
    home = lax.div(f, SIDE)

    def to(du, df):
        return {"uly": du, "fsdp": df}

    def remote(src, dst, send, recv, device):
        return pltpu.make_async_remote_copy(
            src_ref=src, dst_ref=dst, send_sem=send, recv_sem=recv,
            device_id=device, device_id_type=MESH,
        )

    def drain(ref, sem):
        pltpu.make_async_copy(ref, ref, sem).wait()

    def span(start, size):
        return pl.ds(pl.multiple_of(start, size), size)

    def ring(offset):
        return lax.rem(u + offset, ULY)

    place = (x, y)

    def along(axis, offset):
        return lax.rem(place[axis] + offset, SIDE)

    def mate(axis, offset):
        return SIDE * y + along(0, offset) if axis == 0 else SIDE * along(1, offset) + x

    def pick(half, for_first, for_second):
        return jnp.where(half == 0, for_first, for_second)

    barrier = pltpu.get_barrier_semaphore()

    def greet(device):
        pl.semaphore_signal(barrier, inc=1, device_id=device, device_id_type=MESH)

    for d in range(1, ULY):
        greet(to(ring(d), f))
    for d in range(ULY):
        greet(to(ring(d), other))
    for source_z in range(SIDE):
        source = 2 * source_z + home
        pl.when(source != f)(lambda source=source: greet(to(u, source)))

    def kv_here(s):
        return kv.at[:, 0, y] if s == 0 else kv.at[:, 1, :, x]

    def send_heads(s, d):
        target = along(s, d)
        cols = span(target * GROUP * HD, GROUP * HD)
        for which, hbm in enumerate((q_hbm, g_hbm)):
            src, dst = hbm.at[s, :, cols], qg.at[s, place[s], which]
            if d == 0:
                pltpu.make_async_copy(src, dst, q_recv.at[s, d]).start()
            else:
                remote(src, dst, q_send.at[s], q_recv.at[s, d], to(mate(s, d), f)).start()

    def send_kv(s, d):
        cols = span(along(s, d) * HD, HD)
        for which, hbm in enumerate((k_hbm, v_hbm)):
            src, dst = hbm.at[s, :, cols], kv.at[which, s, y, x]
            if d == 0:
                pltpu.make_async_copy(src, dst, kv_recv.at[s]).start()
            else:
                remote(src, dst, kv_send.at[s], kv_recv.at[s], to(mate(s, d), f)).start()

    def send_inputs(same, d):
        half = c if same else 1 - c
        own = pick(half, x, y)
        target = lax.rem(own + d, SIDE)
        device = to(pick(half, mate(0, d), mate(1, d)), 2 * z + half)
        for slab in range(SIDE):
            start = pick(half, (slab * SIDE + target) * 2, (target * SIDE + slab) * 2 + 1)
            src = x_hbm.at[:, :, span(start * SLAB, SLAB)]
            dst = xr.at[:, 0 if same else 1, own, :, pl.ds(slab * SLAB, SLAB)]
            if same and d == 0:
                pltpu.make_async_copy(src, dst, x_recv).start()
            else:
                remote(src, dst, x_send.at[0 if same else 1], x_recv, device).start()

    for s in range(SEQ):
        send_kv(s, 0)
    for s in range(SEQ):
        send_heads(s, 0)
    send_inputs(True, 0)
    pl.semaphore_wait(barrier, 2 * ULY - 1 + SIDE - jnp.where(home == c, 1, 0))
    def share_kv(s):
        drain(kv_here(s), kv_recv.at[s])
        for d in range(1, SIDE):
            def send(d=d):
                remote(
                    kv_here(s), kv_here(s), kv_all_send.at[s, d], kv_all_recv.at[s, d],
                    to(mate(1 - s, d), f),
                ).start()

            if s == 0:
                pl.when(y + d < SIDE)(send)
            else:
                send()

    def kv_shared(s):
        for d in range(1, SIDE):
            def wait(d=d):
                drain(kv.at[:, s, 0], kv_all_recv.at[s, d])

            if s == 0:
                pl.when(y >= d)(wait)
            else:
                wait()

    def kv_left(s):
        for d in range(1, SIDE):
            def wait(d=d):
                drain(kv.at[:, s, 0], kv_all_send.at[s, d])

            if s == 0:
                pl.when(y + d < SIDE)(wait)
            else:
                wait()

    def send_all_inputs():
        for d in range(SIDE):
            if d:
                send_inputs(True, d)
            send_inputs(False, d)

    for s in range(SEQ):
        for d in range(1, SIDE):
            send_kv(s, d)
    for d in range(1, SIDE):
        for s in range(SEQ):
            send_heads(s, d)
    dkacc[...] = jnp.zeros_like(dkacc)
    for s in range(SEQ):
        share_kv(s)
    if INPUTS_AFTER < 0:
        send_all_inputs()

    rows = GROUP * TOK
    chunk = SIDE * TOK

    def heads_to_rows(block):
        return jnp.concatenate([block[:, h * HD:(h + 1) * HD] for h in range(GROUP)], axis=0)

    def nt(a, b):
        return lax.dot_general(a, b, (((1,), (1,)), ((), ())), preferred_element_type=jnp.float32)

    def attend_to(s, slot, chunks, block_x):
        query = heads_to_rows(qg[s, slot, 0])
        grad = heads_to_rows(qg[s, slot, 1])
        key_at = lax.broadcasted_iota(jnp.int32, (chunk, rows), 0)
        query_at = lax.rem(lax.broadcasted_iota(jnp.int32, (chunk, rows), 1), TOK)
        scores = []
        for n in range(chunks):
            keys = kv[0, s, n].reshape(chunk, HD)
            scores.append(nt(keys, query) * (SCALE * LOG2E))
        scores[-1] = jnp.where(key_at > query_at + block_x * TOK, -jnp.inf, scores[-1])
        top_score = jnp.max(scores[0], axis=0, keepdims=True)
        for block in scores[1:]:
            top_score = jnp.maximum(top_score, jnp.max(block, axis=0, keepdims=True))
        exps = [jnp.exp2(block - top_score) for block in scores]
        prob_grads = []
        for n in range(chunks):
            values = kv[1, s, n].reshape(chunk, HD)
            prob_grads.append(nt(values, grad))
        total = sum(jnp.sum(e, axis=0, keepdims=True) for e in exps)
        weighted = sum(jnp.sum(e * p, axis=0, keepdims=True) for e, p in zip(exps, prob_grads))
        row_terms = weighted / total
        scale = SCALE / total
        for n in range(chunks):
            score_grad = (exps[n] * ((prob_grads[n] - row_terms) * scale)).astype(jnp.bfloat16)
            term = jnp.dot(score_grad, query, preferred_element_type=jnp.float32)
            dkacc[s, n] += term.reshape(SIDE, TOK, HD)

    def send_partials():
        part[0] = dkacc[0].astype(jnp.bfloat16)
        for d in range(1, SIDE):
            remote(
                part.at[0, along(1, d)], part_in.at[0, d - 1],
                part_send, part_recv, to(mate(1, d), f),
            ).start()

    def send_chunk(n):
        part[1, :, n] = dkacc[1, n].astype(jnp.bfloat16)
        for d in range(1, SIDE):
            remote(
                part.at[1, along(0, d), n], part_in.at[1, d - 1, n],
                chunk_send.at[n], chunk_recv.at[n], to(mate(0, d), f),
            ).start()

    def give(s, half, src, slot, device, here, send):
        cols = span(place[s] * HD, HD)
        dst = dka.at[s, jnp.where(c == half, 0, 1), slot, :, cols]

        def away():
            remote(src, dst, send, dk_recv.at[s], device).start()

        def stay():
            pltpu.make_async_copy(src, dst, dk_recv.at[s]).start()

        if here is None:
            away()
        else:
            own = jnp.logical_and(here, c == half)
            pl.when(own)(stay)
            pl.when(jnp.logical_not(own))(away)

    def widest(summed):
        return jnp.max(jnp.abs(summed).reshape(-1, 8, HD), axis=0)

    def send_key_grad():
        drain(part_in.at[0], part_recv)
        summed = dkacc[0, y]
        for d in range(SIDE - 1):
            summed += part_in[0, d].astype(jnp.float32)
        dkf[0] = summed.astype(jnp.bfloat16)
        top[...] = widest(summed)
        for d in range(ULY):
            give(
                0, 1, dkf.at[0, lax.rem(ring(d), SIDE)], y, to(ring(d), 2 * z + 1),
                True if d == 0 else None, dk_send.at[0, 1],
            )
        for d in range(SIDE):
            give(
                0, 0, dkf.at[0], slice(None), to(mate(0, d), 2 * z),
                True if d == 0 else None, dk_send.at[0, 0],
            )

    def send_key_grad_chunk(n):
        drain(part_in.at[1, 0:SIDE - 1, n], chunk_recv.at[n])
        summed = dkacc[1, n, x]
        for d in range(SIDE - 1):
            summed += part_in[1, d, n].astype(jnp.float32)
        dkf[1, n] = summed.astype(jnp.bfloat16)
        top[...] = jnp.maximum(top[...], widest(summed))
        for d in range(SIDE):
            give(
                1, 0, dkf.at[1, n], x, to(SIDE * n + along(0, d), 2 * z),
                y == n if d == 0 else None, dk_send.at[1, 1],
            )
            give(
                1, 1, dkf.at[1, n], n, to(mate(1, d), 2 * z + 1),
                True if d == 0 else None, dk_send.at[1, 0],
            )

    def grad_rows(s, cols):
        return dka[s, :, :, :, cols].reshape(2 * SIDE * TOK, -1)

    kv_shared(0)

    def step(i, carry):
        d = i
        slot = lax.rem(x - d + SIDE, SIDE)
        drain(qg.at[0, slot], q_recv.at[0, d])
        for chunks in range(1, SIDE + 1):
            pl.when(y == chunks - 1)(functools.partial(attend_to, 0, slot, chunks, slot))
        if INPUTS_AFTER >= 0:
            pl.when(i == INPUTS_AFTER)(send_all_inputs)
        return carry

    lax.fori_loop(0, SIDE, step, 0)
    send_partials()
    kv_shared(1)
    for n in reversed(range(SIDE)):
        drain(qg.at[1, n], q_recv.at[1, lax.rem(y - n + SIDE, SIDE)])
        attend_to(1, n, n + 1, x)
        send_chunk(n)
        if n == GRAD_BEFORE:
            send_key_grad()
    for n in reversed(range(SIDE)):
        send_key_grad_chunk(n)

    drain(xr, x_recv)
    input_max = jnp.float32(0.0)
    for s in range(SEQ):
        block = xr[s].reshape(2 * SIDE * TOK, BAND)
        tops = jnp.max(jnp.abs(block), axis=0, keepdims=True).astype(jnp.float32)
        input_max = jnp.maximum(input_max, jnp.max(tops))
        xt[s] = block.T
    key_max = jnp.max(top[...])
    row_at = lax.broadcasted_iota(jnp.int32, (8, HD), 0)
    m_own[...] = jnp.where(row_at < 4, input_max, key_max)
    for dc in range(2):
        for d in range(SIDE):
            if dc or d:
                remote(
                    m_own, m_row.at[dc * SIDE + d - 1], m_send.at[0], m_recv.at[0],
                    to(mate(0, d), f if dc == 0 else other),
                ).start()
    drain(dka.at[0], dk_recv.at[0])
    acc[...] = jnp.dot(xt[0], grad_rows(0, slice(None)), preferred_element_type=jnp.float32)
    drain(m_row, m_recv.at[0])
    m_y_out[...] = jnp.maximum(m_own[...], jnp.max(m_row[...], axis=0))
    for d in range(1, SIDE):
        remote(
            m_y_out, m_y_in.at[d - 1], m_send.at[1], m_recv.at[1], to(mate(1, d), f)
        ).start()
    drain(dka.at[1], dk_recv.at[1])

    own = pick(c, y, x)

    def slab_grad(target, cols):
        at = span(target * SLAB, SLAB)
        return acc[at, cols] + jnp.dot(
            xt[1, at], grad_rows(1, cols), preferred_element_type=jnp.float32
        )

    parts = [slice(p * PART, (p + 1) * PART) for p in range(COLS // PART)]
    for p, cols in enumerate(parts):
        for d in range(1, SIDE):
            y_out[p, d - 1] = slab_grad(lax.rem(own + d, SIDE), cols).astype(jnp.bfloat16)
            remote(
                y_out.at[p, d - 1], y_in.at[p, d - 1], y_send.at[p], y_recv.at[p],
                to(pick(c, mate(1, d), mate(0, d)), f),
            ).start()
    sums = [slab_grad(own, cols) for cols in parts]
    drain(m_y_in, m_recv.at[1])
    m_z_out[...] = jnp.maximum(m_y_out[...], jnp.max(m_y_in[...], axis=0))

    def last_sends(k, src, dst, send, recv):
        target = SIDE * c + k

        def away():
            remote(src, dst, send, recv, to(u, target)).start()

        def stay():
            pltpu.make_async_copy(src, dst, recv).start()

        pl.when(target != f)(away)
        pl.when(target == f)(stay)

    for k in range(SIDE):
        last_sends(k, m_z_out, m_z_in.at[z], m_send.at[2], m_recv.at[2])
    for p in range(len(parts)):
        drain(y_in.at[p], y_recv.at[p])
        for d in range(SIDE - 1):
            sums[p] += y_in[p, d].astype(jnp.float32)
        z_out[p] = sums[p].reshape(SIDE, OUT_ROWS, PART).astype(jnp.bfloat16)
        for k in range(SIDE):
            last_sends(k, z_out.at[p, k], z_in.at[p, z], z_send.at[p], z_recv.at[p])
    drain(m_z_in, m_recv.at[2])
    largest = jnp.max(m_z_in[...], axis=0)
    input_top = jnp.max(largest[0:4], axis=0, keepdims=True)[:, 0:1]
    key_top = jnp.max(largest[4:8], axis=0, keepdims=True)[:, 0:1]
    factor = 36.0 / (input_top * key_top) / math.sqrt(SEQ * FSDP * ULY * TOK)
    for p, cols in enumerate(parts):
        drain(z_in.at[p], z_recv.at[p])
        raw = z_in[p, 0].astype(jnp.float32)
        for source_z in range(1, SIDE):
            raw += z_in[p, source_z].astype(jnp.float32)
        out_ref[:, cols] = (raw * factor).astype(jnp.bfloat16)

    for s in range(SEQ):
        drain(kv.at[:, s, 0, 0:SIDE - 1], kv_send.at[s])

        def drain_same(s=s):
            drain(part_in.at[s], dk_send.at[s, 0])
            drain(part.at[s], dk_send.at[s, 1])

        def drain_other(s=s):
            drain(part.at[s], dk_send.at[s, 0])
            drain(xt.at[s, 0:(ULY - 1) * TOK * HD // (2 * SIDE * TOK)], dk_send.at[s, 1])

        pl.when(c == s)(drain_same)
        pl.when(c != s)(drain_other)
    drain(qg.at[1, 0:SIDE - 1], q_send.at[1])
    kv_left(1)
    drain(part_in.at[0], part_send)
    drain(qg.at[0, 0:SIDE - 1], q_send.at[0])
    kv_left(0)
    for n in range(SIDE):
        drain(part_in.at[1, 0:SIDE - 1, n], chunk_send.at[n])
    drain(xr.at[:, 0, 0:SIDE - 1], x_send.at[0])
    drain(xr.at[:, 1], x_send.at[1])
    for p in range(len(parts)):
        drain(y_in.at[p], y_send.at[p])
    drain(m_row, m_send.at[0])
    drain(m_y_in, m_send.at[1])

    def drain_last(count):
        for p in range(len(parts)):
            drain(z_in.at[p, 0:count], z_send.at[p])
        drain(m_z_in.at[0:count], m_send.at[2])

    pl.when(home == c)(lambda: drain_last(SIDE - 1))
    pl.when(home != c)(lambda: drain_last(SIDE))


def per_device(inputs_norm, queries, key_states, value_states, context_grad):
    bf16, f32 = jnp.bfloat16, jnp.float32
    parts = COLS // PART
    vmem, dma = pltpu.VMEM, pltpu.SemaphoreType.DMA
    return pl.pallas_call(
        kernel,
        out_shape=jax.ShapeDtypeStruct((OUT_ROWS, COLS), bf16),
        in_specs=[pl.BlockSpec(memory_space=pl.ANY)] * 5,
        out_specs=pl.BlockSpec(memory_space=pltpu.VMEM),
        scratch_shapes=[
            vmem((SEQ, SIDE, 2, TOK, GROUP * HD), bf16),
            vmem((2, SEQ, SIDE, SIDE, TOK, HD), bf16),
            vmem((SEQ, 2, SIDE, TOK, BAND), bf16),
            vmem((SEQ, BAND, 2 * SIDE * TOK), bf16),
            vmem((SEQ, SIDE, SIDE, TOK, HD), f32),
            vmem((SEQ, SIDE, SIDE, TOK, HD), bf16),
            vmem((SEQ, SIDE - 1, SIDE, TOK, HD), bf16),
            vmem((SEQ, SIDE, TOK, HD), bf16),
            vmem((SEQ, 2, SIDE, TOK, COLS), bf16),
            vmem((BAND, COLS), f32),
            vmem((parts, SIDE - 1, SLAB, PART), bf16),
            vmem((parts, SIDE - 1, SLAB, PART), bf16),
            vmem((parts, SIDE, OUT_ROWS, PART), bf16),
            vmem((parts, SIDE, OUT_ROWS, PART), bf16),
            vmem((8, HD), f32),
            vmem((8, HD), f32),
            vmem((2 * SIDE - 1, 8, HD), f32),
            vmem((8, HD), f32),
            vmem((SIDE - 1, 8, HD), f32),
            vmem((8, HD), f32),
            vmem((SIDE, 8, HD), f32),
            dma((SEQ, SIDE)), dma((SEQ,)), dma((SEQ, SIDE)), dma, dma, dma((SIDE,)),
            dma((SEQ,)), dma((parts,)), dma((parts,)), dma((3,)),
            dma((SEQ,)), dma((SEQ,)), dma((SEQ, SIDE)), dma((2,)), dma, dma((SIDE,)),
            dma((SEQ, 2)), dma((parts,)), dma((parts,)), dma((3,)),
        ],
        compiler_params=pltpu.CompilerParams(
            collective_id=0, has_side_effects=True, vmem_limit_bytes=56 * 1024 * 1024
        ),
    )(inputs_norm, queries, key_states, value_states, context_grad)


def solution(mesh):
    placed = P(("rep", "fsdp"), "uly", None)
    return jax.shard_map(
        per_device,
        mesh=mesh,
        in_specs=(placed,) * 5,
        out_specs=P(("rep", "uly", "fsdp"), None),
        check_vma=False,
    )
```

```python
import functools
import math

import jax
import jax.numpy as jnp
from jax import lax
from jax.experimental import pallas as pl
from jax.experimental.pallas import tpu as pltpu
from jax.sharding import PartitionSpec as P

MESH = pl.DeviceIdType.MESH
KVH = 4
HD = 128
SIDE = 4
ULY = SIDE * SIDE
FSDP = 8
SEQ = 2
TOK = 64
GROUP = 8
WIDTH = 8192
BAND = 1024
SLAB = BAND // SIDE
OUT_ROWS = 64
COLS = KVH * HD
EARLY = (0, 1)
HEADS = (1, 2, 3)
INPUTS_AFTER = 0
GRAD_AFTER = 2
FAR_FIRST = (2, 1, 3)
PART = 128
SCALE = 1.0 / math.sqrt(HD)
LOG2E = math.log2(math.e)


def kernel(
    x_hbm, q_hbm, k_hbm, v_hbm, g_hbm, out_ref,
    qg, kv, xr, xt, dkacc, part, part_in, dkf, dka, acc,
    y_out, y_in, z_out, z_in, top, m_own, m_row, m_y_out, m_y_in, m_z_out, m_z_in,
    q_recv, kv_recv, kv_all_recv, x_recv, part_recv, chunk_recv, dk_recv, y_recv, z_recv, m_recv,
    q_send, kv_send, kv_all_send, x_send, part_send, chunk_send, dk_send, y_send, z_send, m_send,
):
    u = lax.axis_index("uly")
    f = lax.axis_index("fsdp")
    y, x = lax.div(u, SIDE), lax.rem(u, SIDE)
    z, c = lax.div(f, 2), lax.rem(f, 2)
    other = 2 * z + 1 - c
    home = lax.div(f, SIDE)

    def to(du, df):
        return {"uly": du, "fsdp": df}

    def remote(src, dst, send, recv, device):
        return pltpu.make_async_remote_copy(
            src_ref=src, dst_ref=dst, send_sem=send, recv_sem=recv,
            device_id=device, device_id_type=MESH,
        )

    def drain(ref, sem):
        pltpu.make_async_copy(ref, ref, sem).wait()

    def span(start, size):
        return pl.ds(pl.multiple_of(start, size), size)

    def ring(offset):
        return lax.rem(u + offset, ULY)

    place = (x, y)

    def along(axis, offset):
        return lax.rem(place[axis] + offset, SIDE)

    def mate(axis, offset):
        return SIDE * y + along(0, offset) if axis == 0 else SIDE * along(1, offset) + x

    def pick(half, for_first, for_second):
        return jnp.where(half == 0, for_first, for_second)

    barrier = pltpu.get_barrier_semaphore()

    def greet(device):
        pl.semaphore_signal(barrier, inc=1, device_id=device, device_id_type=MESH)

    for d in range(1, ULY):
        greet(to(ring(d), f))
    for d in range(ULY):
        greet(to(ring(d), other))
    for source_z in range(SIDE):
        source = 2 * source_z + home
        pl.when(source != f)(lambda source=source: greet(to(u, source)))

    def kv_here(s):
        return kv.at[:, 0, y] if s == 0 else kv.at[:, 1, :, x]

    def send_heads(s, d):
        target = along(s, d)
        cols = span(target * GROUP * HD, GROUP * HD)
        for which, hbm in enumerate((q_hbm, g_hbm)):
            src, dst = hbm.at[s, :, cols], qg.at[s, place[s], which]
            if d == 0:
                pltpu.make_async_copy(src, dst, q_recv.at[s, d]).start()
            else:
                remote(src, dst, q_send.at[s], q_recv.at[s, d], to(mate(s, d), f)).start()

    def send_kv(s, d):
        cols = span(along(s, d) * HD, HD)
        for which, hbm in enumerate((k_hbm, v_hbm)):
            src, dst = hbm.at[s, :, cols], kv.at[which, s, y, x]
            if d == 0:
                pltpu.make_async_copy(src, dst, kv_recv.at[s]).start()
            else:
                remote(src, dst, kv_send.at[s], kv_recv.at[s], to(mate(s, d), f)).start()

    def send_inputs(same, d):
        half = c if same else 1 - c
        own = pick(half, x, y)
        target = lax.rem(own + d, SIDE)
        device = to(pick(half, mate(0, d), mate(1, d)), 2 * z + half)
        for slab in range(SIDE):
            start = pick(half, (slab * SIDE + target) * 2, (target * SIDE + slab) * 2 + 1)
            src = x_hbm.at[:, :, span(start * SLAB, SLAB)]
            dst = xr.at[:, 0 if same else 1, own, :, pl.ds(slab * SLAB, SLAB)]
            if same and d == 0:
                pltpu.make_async_copy(src, dst, x_recv).start()
            else:
                remote(src, dst, x_send.at[0 if same else 1], x_recv, device).start()

    for s in range(SEQ):
        send_kv(s, 0)
    for s in range(SEQ):
        send_heads(s, 0)
    send_inputs(True, 0)
    pl.semaphore_wait(barrier, 2 * ULY - 1 + SIDE - jnp.where(home == c, 1, 0))
    def share_kv(s):
        drain(kv_here(s), kv_recv.at[s])
        for d in FAR_FIRST:
            def send(d=d):
                remote(
                    kv_here(s), kv_here(s), kv_all_send.at[s, d], kv_all_recv.at[s, d],
                    to(mate(1 - s, d), f),
                ).start()

            if s == 0:
                pl.when(y + d < SIDE)(send)
            else:
                send()

    def kv_shared(s):
        for d in range(1, SIDE):
            def wait(d=d):
                drain(kv.at[:, s, 0], kv_all_recv.at[s, d])

            if s == 0:
                pl.when(y >= d)(wait)
            else:
                wait()

    def kv_left(s):
        for d in range(1, SIDE):
            def wait(d=d):
                drain(kv.at[:, s, 0], kv_all_send.at[s, d])

            if s == 0:
                pl.when(y + d < SIDE)(wait)
            else:
                wait()

    def send_all_inputs(offsets):
        for d in offsets:
            if d:
                send_inputs(True, d)
            send_inputs(False, d)

    for s in range(SEQ):
        for d in FAR_FIRST:
            send_kv(s, d)
    for d in HEADS:
        for s in range(SEQ):
            send_heads(s, d)
    dkacc[...] = jnp.zeros_like(dkacc)
    top[...] = jnp.zeros_like(top)
    for s in range(SEQ):
        share_kv(s)
    send_all_inputs(EARLY)

    rows = GROUP * TOK
    chunk = SIDE * TOK

    def heads_to_rows(block):
        return jnp.concatenate([block[:, h * HD:(h + 1) * HD] for h in range(GROUP)], axis=0)

    def nt(a, b):
        return lax.dot_general(a, b, (((1,), (1,)), ((), ())), preferred_element_type=jnp.float32)

    def attend_to(s, slot, chunks, block_x):
        query = heads_to_rows(qg[s, slot, 0])
        grad = heads_to_rows(qg[s, slot, 1])
        key_at = lax.broadcasted_iota(jnp.int32, (chunk, rows), 0)
        query_at = lax.rem(lax.broadcasted_iota(jnp.int32, (chunk, rows), 1), TOK)
        scores = []
        for n in range(chunks):
            keys = kv[0, s, n].reshape(chunk, HD)
            scores.append(nt(keys, query) * (SCALE * LOG2E))
        scores[-1] = jnp.where(key_at > query_at + block_x * TOK, -jnp.inf, scores[-1])
        top_score = jnp.max(scores[0], axis=0, keepdims=True)
        for block in scores[1:]:
            top_score = jnp.maximum(top_score, jnp.max(block, axis=0, keepdims=True))
        exps = [jnp.exp2(block - top_score) for block in scores]
        prob_grads = []
        for n in range(chunks):
            values = kv[1, s, n].reshape(chunk, HD)
            prob_grads.append(nt(values, grad))
        total = sum(jnp.sum(e, axis=0, keepdims=True) for e in exps)
        weighted = sum(jnp.sum(e * p, axis=0, keepdims=True) for e, p in zip(exps, prob_grads))
        row_terms = weighted / total
        scale = SCALE / total
        for n in range(chunks):
            score_grad = (exps[n] * ((prob_grads[n] - row_terms) * scale)).astype(jnp.bfloat16)
            term = jnp.dot(score_grad, query, preferred_element_type=jnp.float32)
            dkacc[s, n] += term.reshape(SIDE, TOK, HD)

    def send_partials():
        part[0] = dkacc[0].astype(jnp.bfloat16)
        for d in FAR_FIRST:
            remote(
                part.at[0, along(1, d)], part_in.at[0, d - 1],
                part_send, part_recv, to(mate(1, d), f),
            ).start()

    def send_chunk(n):
        part[1, :, n] = dkacc[1, n].astype(jnp.bfloat16)
        for d in FAR_FIRST:
            remote(
                part.at[1, along(0, d), n], part_in.at[1, d - 1, n],
                chunk_send.at[n], chunk_recv.at[n], to(mate(0, d), f),
            ).start()

    def give(s, half, src, slot, device, here, send):
        cols = span(place[s] * HD, HD)
        dst = dka.at[s, jnp.where(c == half, 0, 1), slot, :, cols]

        def away():
            remote(src, dst, send, dk_recv.at[s], device).start()

        def stay():
            pltpu.make_async_copy(src, dst, dk_recv.at[s]).start()

        if here is None:
            away()
        else:
            own = jnp.logical_and(here, c == half)
            pl.when(own)(stay)
            pl.when(jnp.logical_not(own))(away)

    def widest(summed):
        return jnp.max(jnp.abs(summed).reshape(-1, 8, HD), axis=0)

    def send_key_grad():
        drain(part_in.at[0], part_recv)
        summed = dkacc[0, y]
        for d in range(SIDE - 1):
            summed += part_in[0, d].astype(jnp.float32)
        dkf[0] = summed.astype(jnp.bfloat16)
        top[...] = jnp.maximum(top[...], widest(summed))
        for d in (10, 6, 9, 11, 14, 2, 8, 5, 7, 13, 15, 1, 3, 4, 12, 0):
            give(
                0, 1, dkf.at[0, lax.rem(ring(d), SIDE)], y, to(ring(d), 2 * z + 1),
                True if d == 0 else None, dk_send.at[0, 1],
            )
        for d in (*FAR_FIRST, 0):
            give(
                0, 0, dkf.at[0], slice(None), to(mate(0, d), 2 * z),
                True if d == 0 else None, dk_send.at[0, 0],
            )

    def send_key_grad_chunk(n):
        drain(part_in.at[1, 0:SIDE - 1, n], chunk_recv.at[n])
        summed = dkacc[1, n, x]
        for d in range(SIDE - 1):
            summed += part_in[1, d, n].astype(jnp.float32)
        dkf[1, n] = summed.astype(jnp.bfloat16)
        top[...] = jnp.maximum(top[...], widest(summed))
        for d in (*FAR_FIRST, 0):
            give(
                1, 0, dkf.at[1, n], x, to(SIDE * n + along(0, d), 2 * z),
                y == n if d == 0 else None, dk_send.at[1, 1],
            )
            give(
                1, 1, dkf.at[1, n], n, to(mate(1, d), 2 * z + 1),
                True if d == 0 else None, dk_send.at[1, 0],
            )

    def grad_rows(s, cols):
        return dka[s, :, :, :, cols].reshape(2 * SIDE * TOK, -1)

    kv_shared(0)

    def step(i, carry):
        d = i
        slot = lax.rem(x - d + SIDE, SIDE)
        drain(qg.at[0, slot], q_recv.at[0, d])
        for chunks in range(1, SIDE + 1):
            pl.when(y == chunks - 1)(functools.partial(attend_to, 0, slot, chunks, slot))
        late = [d for d in range(SIDE) if d not in EARLY]
        pl.when(i == INPUTS_AFTER)(lambda: send_all_inputs(late))
        return carry

    lax.fori_loop(0, SIDE, step, 0)
    send_partials()
    kv_shared(1)
    for n in reversed(range(SIDE)):
        drain(qg.at[1, n], q_recv.at[1, lax.rem(y - n + SIDE, SIDE)])
        attend_to(1, n, n + 1, x)
        send_chunk(n)
    for n in reversed(range(SIDE)):
        send_key_grad_chunk(n)
        if n == GRAD_AFTER:
            send_key_grad()

    drain(xr, x_recv)
    input_max = jnp.float32(0.0)
    for s in range(SEQ):
        block = xr[s].reshape(2 * SIDE * TOK, BAND)
        tops = jnp.max(jnp.abs(block), axis=0, keepdims=True).astype(jnp.float32)
        input_max = jnp.maximum(input_max, jnp.max(tops))
        xt[s] = block.T
    key_max = jnp.max(top[...])
    row_at = lax.broadcasted_iota(jnp.int32, (8, HD), 0)
    m_own[...] = jnp.where(row_at < 4, input_max, key_max)
    for dc in range(2):
        for d in range(SIDE):
            if dc or d:
                remote(
                    m_own, m_row.at[dc * SIDE + d - 1], m_send.at[0], m_recv.at[0],
                    to(mate(0, d), f if dc == 0 else other),
                ).start()
    drain(dka.at[0], dk_recv.at[0])
    acc[...] = jnp.dot(xt[0], grad_rows(0, slice(None)), preferred_element_type=jnp.float32)
    drain(m_row, m_recv.at[0])
    m_y_out[...] = jnp.maximum(m_own[...], jnp.max(m_row[...], axis=0))
    for d in range(1, SIDE):
        remote(
            m_y_out, m_y_in.at[d - 1], m_send.at[1], m_recv.at[1], to(mate(1, d), f)
        ).start()
    drain(dka.at[1], dk_recv.at[1])

    own = pick(c, y, x)

    def slab_grad(target, cols):
        at = span(target * SLAB, SLAB)
        return acc[at, cols] + jnp.dot(
            xt[1, at], grad_rows(1, cols), preferred_element_type=jnp.float32
        )

    parts = [slice(p * PART, (p + 1) * PART) for p in range(COLS // PART)]
    for p, cols in enumerate(parts):
        for d in FAR_FIRST:
            y_out[p, d - 1] = slab_grad(lax.rem(own + d, SIDE), cols).astype(jnp.bfloat16)
            remote(
                y_out.at[p, d - 1], y_in.at[p, d - 1], y_send.at[p], y_recv.at[p],
                to(pick(c, mate(1, d), mate(0, d)), f),
            ).start()
    sums = [slab_grad(own, cols) for cols in parts]
    drain(m_y_in, m_recv.at[1])
    m_z_out[...] = jnp.maximum(m_y_out[...], jnp.max(m_y_in[...], axis=0))

    def last_sends(k, src, dst, send, recv):
        target = SIDE * c + k

        def away():
            remote(src, dst, send, recv, to(u, target)).start()

        def stay():
            pltpu.make_async_copy(src, dst, recv).start()

        pl.when(target != f)(away)
        pl.when(target == f)(stay)

    for k in range(SIDE):
        last_sends(k, m_z_out, m_z_in.at[z], m_send.at[2], m_recv.at[2])
    for p in range(len(parts)):
        drain(y_in.at[p], y_recv.at[p])
        for d in range(SIDE - 1):
            sums[p] += y_in[p, d].astype(jnp.float32)
        z_out[p] = sums[p].reshape(SIDE, OUT_ROWS, PART).astype(jnp.bfloat16)
        for k in range(SIDE):
            last_sends(k, z_out.at[p, k], z_in.at[p, z], z_send.at[p], z_recv.at[p])
    drain(m_z_in, m_recv.at[2])
    largest = jnp.max(m_z_in[...], axis=0)
    input_top = jnp.max(largest[0:4], axis=0, keepdims=True)[:, 0:1]
    key_top = jnp.max(largest[4:8], axis=0, keepdims=True)[:, 0:1]
    factor = 36.0 / (input_top * key_top) / math.sqrt(SEQ * FSDP * ULY * TOK)
    for p, cols in enumerate(parts):
        drain(z_in.at[p], z_recv.at[p])
        raw = z_in[p, 0].astype(jnp.float32)
        for source_z in range(1, SIDE):
            raw += z_in[p, source_z].astype(jnp.float32)
        out_ref[:, cols] = (raw * factor).astype(jnp.bfloat16)

    for s in range(SEQ):
        drain(kv.at[:, s, 0, 0:SIDE - 1], kv_send.at[s])

        def drain_same(s=s):
            drain(part_in.at[s], dk_send.at[s, 0])
            drain(part.at[s], dk_send.at[s, 1])

        def drain_other(s=s):
            drain(part.at[s], dk_send.at[s, 0])
            drain(xt.at[s, 0:(ULY - 1) * TOK * HD // (2 * SIDE * TOK)], dk_send.at[s, 1])

        pl.when(c == s)(drain_same)
        pl.when(c != s)(drain_other)
    drain(qg.at[1, 0:SIDE - 1], q_send.at[1])
    kv_left(1)
    drain(part_in.at[0], part_send)
    drain(qg.at[0, 0:SIDE - 1], q_send.at[0])
    kv_left(0)
    for n in range(SIDE):
        drain(part_in.at[1, 0:SIDE - 1, n], chunk_send.at[n])
    drain(xr.at[:, 0, 0:SIDE - 1], x_send.at[0])
    drain(xr.at[:, 1], x_send.at[1])
    for p in range(len(parts)):
        drain(y_in.at[p], y_send.at[p])
    drain(m_row, m_send.at[0])
    drain(m_y_in, m_send.at[1])

    def drain_last(count):
        for p in range(len(parts)):
            drain(z_in.at[p, 0:count], z_send.at[p])
        drain(m_z_in.at[0:count], m_send.at[2])

    pl.when(home == c)(lambda: drain_last(SIDE - 1))
    pl.when(home != c)(lambda: drain_last(SIDE))


def per_device(inputs_norm, queries, key_states, value_states, context_grad):
    bf16, f32 = jnp.bfloat16, jnp.float32
    parts = COLS // PART
    vmem, dma = pltpu.VMEM, pltpu.SemaphoreType.DMA
    return pl.pallas_call(
        kernel,
        out_shape=jax.ShapeDtypeStruct((OUT_ROWS, COLS), bf16),
        in_specs=[pl.BlockSpec(memory_space=pl.ANY)] * 5,
        out_specs=pl.BlockSpec(memory_space=pltpu.VMEM),
        scratch_shapes=[
            vmem((SEQ, SIDE, 2, TOK, GROUP * HD), bf16),
            vmem((2, SEQ, SIDE, SIDE, TOK, HD), bf16),
            vmem((SEQ, 2, SIDE, TOK, BAND), bf16),
            vmem((SEQ, BAND, 2 * SIDE * TOK), bf16),
            vmem((SEQ, SIDE, SIDE, TOK, HD), f32),
            vmem((SEQ, SIDE, SIDE, TOK, HD), bf16),
            vmem((SEQ, SIDE - 1, SIDE, TOK, HD), bf16),
            vmem((SEQ, SIDE, TOK, HD), bf16),
            vmem((SEQ, 2, SIDE, TOK, COLS), bf16),
            vmem((BAND, COLS), f32),
            vmem((parts, SIDE - 1, SLAB, PART), bf16),
            vmem((parts, SIDE - 1, SLAB, PART), bf16),
            vmem((parts, SIDE, OUT_ROWS, PART), bf16),
            vmem((parts, SIDE, OUT_ROWS, PART), bf16),
            vmem((8, HD), f32),
            vmem((8, HD), f32),
            vmem((2 * SIDE - 1, 8, HD), f32),
            vmem((8, HD), f32),
            vmem((SIDE - 1, 8, HD), f32),
            vmem((8, HD), f32),
            vmem((SIDE, 8, HD), f32),
            dma((SEQ, SIDE)), dma((SEQ,)), dma((SEQ, SIDE)), dma, dma, dma((SIDE,)),
            dma((SEQ,)), dma((parts,)), dma((parts,)), dma((3,)),
            dma((SEQ,)), dma((SEQ,)), dma((SEQ, SIDE)), dma((2,)), dma, dma((SIDE,)),
            dma((SEQ, 2)), dma((parts,)), dma((parts,)), dma((3,)),
        ],
        compiler_params=pltpu.CompilerParams(
            collective_id=0, has_side_effects=True, vmem_limit_bytes=56 * 1024 * 1024
        ),
    )(inputs_norm, queries, key_states, value_states, context_grad)


def solution(mesh):
    placed = P(("rep", "fsdp"), "uly", None)
    return jax.shard_map(
        per_device,
        mesh=mesh,
        in_specs=(placed,) * 5,
        out_specs=P(("rep", "uly", "fsdp"), None),
        check_vma=False,
    )
```

```python
import functools
import math

import jax
import jax.numpy as jnp
from jax import lax
from jax.experimental import pallas as pl
from jax.experimental.pallas import tpu as pltpu
from jax.sharding import PartitionSpec as P

MESH = pl.DeviceIdType.MESH
KVH = 4
HD = 128
SIDE = 4
ULY = SIDE * SIDE
FSDP = 8
SEQ = 2
TOK = 64
GROUP = 8
WIDTH = 8192
BAND = 1024
SLAB = BAND // SIDE
OUT_ROWS = 64
COLS = KVH * HD
EARLY = (0, 1, 3)
HEADS = (1, 2, 3)
INPUTS_AFTER = 0
GRAD_AFTER = 2
FAR_FIRST = (2, 1, 3)
PART = 128
SCALE = 1.0 / math.sqrt(HD)
LOG2E = math.log2(math.e)


def kernel(
    x_hbm, q_hbm, k_hbm, v_hbm, g_hbm, out_ref,
    qg, kv, xr, xt, dkacc, part, part_in, dkf, dka, acc,
    y_out, y_in, z_out, z_in, top, m_own, m_row, m_y_out, m_y_in, m_z_out, m_z_in,
    q_recv, kv_recv, kv_all_recv, x_recv, part_recv, chunk_recv, dk_recv, y_recv, z_recv, m_recv,
    q_send, kv_send, kv_all_send, x_send, part_send, chunk_send, dk_send, y_send, z_send, m_send,
):
    u = lax.axis_index("uly")
    f = lax.axis_index("fsdp")
    y, x = lax.div(u, SIDE), lax.rem(u, SIDE)
    z, c = lax.div(f, 2), lax.rem(f, 2)
    other = 2 * z + 1 - c
    home = lax.div(f, SIDE)

    def to(du, df):
        return {"uly": du, "fsdp": df}

    def remote(src, dst, send, recv, device):
        return pltpu.make_async_remote_copy(
            src_ref=src, dst_ref=dst, send_sem=send, recv_sem=recv,
            device_id=device, device_id_type=MESH,
        )

    def drain(ref, sem):
        pltpu.make_async_copy(ref, ref, sem).wait()

    def span(start, size):
        return pl.ds(pl.multiple_of(start, size), size)

    def ring(offset):
        return lax.rem(u + offset, ULY)

    place = (x, y)

    def along(axis, offset):
        return lax.rem(place[axis] + offset, SIDE)

    def mate(axis, offset):
        return SIDE * y + along(0, offset) if axis == 0 else SIDE * along(1, offset) + x

    def pick(half, for_first, for_second):
        return jnp.where(half == 0, for_first, for_second)

    barrier = pltpu.get_barrier_semaphore()

    def greet(device):
        pl.semaphore_signal(barrier, inc=1, device_id=device, device_id_type=MESH)

    for d in range(1, ULY):
        greet(to(ring(d), f))
    for d in range(ULY):
        greet(to(ring(d), other))
    for source_z in range(SIDE):
        source = 2 * source_z + home
        pl.when(source != f)(lambda source=source: greet(to(u, source)))

    def kv_here(s):
        return kv.at[:, 0, y] if s == 0 else kv.at[:, 1, :, x]

    def send_heads(s, d):
        target = along(s, d)
        cols = span(target * GROUP * HD, GROUP * HD)
        for which, hbm in enumerate((q_hbm, g_hbm)):
            src, dst = hbm.at[s, :, cols], qg.at[s, place[s], which]
            if d == 0:
                pltpu.make_async_copy(src, dst, q_recv.at[s, d]).start()
            else:
                remote(src, dst, q_send.at[s], q_recv.at[s, d], to(mate(s, d), f)).start()

    def send_kv(s, d):
        cols = span(along(s, d) * HD, HD)
        for which, hbm in enumerate((k_hbm, v_hbm)):
            src, dst = hbm.at[s, :, cols], kv.at[which, s, y, x]
            if d == 0:
                pltpu.make_async_copy(src, dst, kv_recv.at[s]).start()
            else:
                remote(src, dst, kv_send.at[s], kv_recv.at[s], to(mate(s, d), f)).start()

    def send_inputs(same, d):
        half = c if same else 1 - c
        own = pick(half, x, y)
        target = lax.rem(own + d, SIDE)
        device = to(pick(half, mate(0, d), mate(1, d)), 2 * z + half)
        for slab in range(SIDE):
            start = pick(half, (slab * SIDE + target) * 2, (target * SIDE + slab) * 2 + 1)
            src = x_hbm.at[:, :, span(start * SLAB, SLAB)]
            dst = xr.at[:, 0 if same else 1, own, :, pl.ds(slab * SLAB, SLAB)]
            if same and d == 0:
                pltpu.make_async_copy(src, dst, x_recv).start()
            else:
                remote(src, dst, x_send.at[0 if same else 1], x_recv, device).start()

    for s in range(SEQ):
        send_kv(s, 0)
    for s in range(SEQ):
        send_heads(s, 0)
    send_inputs(True, 0)
    pl.semaphore_wait(barrier, 2 * ULY - 1 + SIDE - jnp.where(home == c, 1, 0))
    def share_kv(s):
        drain(kv_here(s), kv_recv.at[s])
        for d in FAR_FIRST:
            def send(d=d):
                remote(
                    kv_here(s), kv_here(s), kv_all_send.at[s, d], kv_all_recv.at[s, d],
                    to(mate(1 - s, d), f),
                ).start()

            if s == 0:
                pl.when(y + d < SIDE)(send)
            else:
                send()

    def kv_shared(s):
        for d in range(1, SIDE):
            def wait(d=d):
                drain(kv.at[:, s, 0], kv_all_recv.at[s, d])

            if s == 0:
                pl.when(y >= d)(wait)
            else:
                wait()

    def kv_left(s):
        for d in range(1, SIDE):
            def wait(d=d):
                drain(kv.at[:, s, 0], kv_all_send.at[s, d])

            if s == 0:
                pl.when(y + d < SIDE)(wait)
            else:
                wait()

    def send_all_inputs(offsets):
        for d in offsets:
            if d:
                send_inputs(True, d)
            send_inputs(False, d)

    for s in range(SEQ):
        for d in FAR_FIRST:
            send_kv(s, d)
    for d in HEADS:
        for s in range(SEQ):
            send_heads(s, d)
    dkacc[...] = jnp.zeros_like(dkacc)
    top[...] = jnp.zeros_like(top)
    for s in range(SEQ):
        share_kv(s)
    send_all_inputs(EARLY)

    rows = GROUP * TOK
    chunk = SIDE * TOK

    def heads_to_rows(block):
        return jnp.concatenate([block[:, h * HD:(h + 1) * HD] for h in range(GROUP)], axis=0)

    def nt(a, b):
        return lax.dot_general(a, b, (((1,), (1,)), ((), ())), preferred_element_type=jnp.float32)

    def attend_to(s, slot, chunks, block_x):
        query = heads_to_rows(qg[s, slot, 0])
        grad = heads_to_rows(qg[s, slot, 1])
        key_at = lax.broadcasted_iota(jnp.int32, (chunk, rows), 0)
        query_at = lax.rem(lax.broadcasted_iota(jnp.int32, (chunk, rows), 1), TOK)
        scores = []
        for n in range(chunks):
            keys = kv[0, s, n].reshape(chunk, HD)
            scores.append(nt(keys, query) * (SCALE * LOG2E))
        scores[-1] = jnp.where(key_at > query_at + block_x * TOK, -jnp.inf, scores[-1])
        top_score = jnp.max(scores[0], axis=0, keepdims=True)
        for block in scores[1:]:
            top_score = jnp.maximum(top_score, jnp.max(block, axis=0, keepdims=True))
        exps = [jnp.exp2(block - top_score) for block in scores]
        prob_grads = []
        for n in range(chunks):
            values = kv[1, s, n].reshape(chunk, HD)
            prob_grads.append(nt(values, grad))
        total = sum(jnp.sum(e, axis=0, keepdims=True) for e in exps)
        weighted = sum(jnp.sum(e * p, axis=0, keepdims=True) for e, p in zip(exps, prob_grads))
        row_terms = weighted / total
        scale = SCALE / total
        for n in range(chunks):
            score_grad = (exps[n] * ((prob_grads[n] - row_terms) * scale)).astype(jnp.bfloat16)
            term = jnp.dot(score_grad, query, preferred_element_type=jnp.float32)
            dkacc[s, n] += term.reshape(SIDE, TOK, HD)

    def send_partials():
        part[0] = dkacc[0].astype(jnp.bfloat16)
        for d in FAR_FIRST:
            remote(
                part.at[0, along(1, d)], part_in.at[0, d - 1],
                part_send, part_recv, to(mate(1, d), f),
            ).start()

    def send_chunk(n):
        part[1, :, n] = dkacc[1, n].astype(jnp.bfloat16)
        for d in FAR_FIRST:
            remote(
                part.at[1, along(0, d), n], part_in.at[1, d - 1, n],
                chunk_send.at[n], chunk_recv.at[n], to(mate(0, d), f),
            ).start()

    def give(s, half, src, slot, device, here, send):
        cols = span(place[s] * HD, HD)
        dst = dka.at[s, jnp.where(c == half, 0, 1), slot, :, cols]

        def away():
            remote(src, dst, send, dk_recv.at[s], device).start()

        def stay():
            pltpu.make_async_copy(src, dst, dk_recv.at[s]).start()

        if here is None:
            away()
        else:
            own = jnp.logical_and(here, c == half)
            pl.when(own)(stay)
            pl.when(jnp.logical_not(own))(away)

    def widest(summed):
        return jnp.max(jnp.abs(summed).reshape(-1, 8, HD), axis=0)

    def send_key_grad():
        drain(part_in.at[0], part_recv)
        summed = dkacc[0, y]
        for d in range(SIDE - 1):
            summed += part_in[0, d].astype(jnp.float32)
        dkf[0] = summed.astype(jnp.bfloat16)
        top[...] = jnp.maximum(top[...], widest(summed))
        for d in (10, 6, 9, 11, 14, 2, 8, 5, 7, 13, 15, 1, 3, 4, 12, 0):
            give(
                0, 1, dkf.at[0, lax.rem(ring(d), SIDE)], y, to(ring(d), 2 * z + 1),
                True if d == 0 else None, dk_send.at[0, 1],
            )
        for d in (*FAR_FIRST, 0):
            give(
                0, 0, dkf.at[0], slice(None), to(mate(0, d), 2 * z),
                True if d == 0 else None, dk_send.at[0, 0],
            )

    def send_key_grad_chunk(n):
        drain(part_in.at[1, 0:SIDE - 1, n], chunk_recv.at[n])
        summed = dkacc[1, n, x]
        for d in range(SIDE - 1):
            summed += part_in[1, d, n].astype(jnp.float32)
        dkf[1, n] = summed.astype(jnp.bfloat16)
        top[...] = jnp.maximum(top[...], widest(summed))
        for d in (*FAR_FIRST, 0):
            give(
                1, 0, dkf.at[1, n], x, to(SIDE * n + along(0, d), 2 * z),
                y == n if d == 0 else None, dk_send.at[1, 1],
            )
            give(
                1, 1, dkf.at[1, n], n, to(mate(1, d), 2 * z + 1),
                True if d == 0 else None, dk_send.at[1, 0],
            )

    def grad_rows(s, cols):
        return dka[s, :, :, :, cols].reshape(2 * SIDE * TOK, -1)

    kv_shared(0)

    def step(i, carry):
        d = i
        slot = lax.rem(x - d + SIDE, SIDE)
        drain(qg.at[0, slot], q_recv.at[0, d])
        for chunks in range(1, SIDE + 1):
            pl.when(y == chunks - 1)(functools.partial(attend_to, 0, slot, chunks, slot))
        late = [d for d in range(SIDE) if d not in EARLY]
        pl.when(i == INPUTS_AFTER)(lambda: send_all_inputs(late))
        return carry

    lax.fori_loop(0, SIDE, step, 0)
    send_partials()
    kv_shared(1)
    for n in reversed(range(SIDE)):
        drain(qg.at[1, n], q_recv.at[1, lax.rem(y - n + SIDE, SIDE)])
        attend_to(1, n, n + 1, x)
        send_chunk(n)
    for n in reversed(range(SIDE)):
        send_key_grad_chunk(n)
        if n == GRAD_AFTER:
            send_key_grad()

    drain(xr, x_recv)
    input_max = jnp.float32(0.0)
    for s in range(SEQ):
        block = xr[s].reshape(2 * SIDE * TOK, BAND)
        tops = jnp.max(jnp.abs(block), axis=0, keepdims=True).astype(jnp.float32)
        input_max = jnp.maximum(input_max, jnp.max(tops))
        xt[s] = block.T
    key_max = jnp.max(top[...])
    row_at = lax.broadcasted_iota(jnp.int32, (8, HD), 0)
    m_own[...] = jnp.where(row_at < 4, input_max, key_max)
    for dc in range(2):
        for d in range(SIDE):
            if dc or d:
                remote(
                    m_own, m_row.at[dc * SIDE + d - 1], m_send.at[0], m_recv.at[0],
                    to(mate(0, d), f if dc == 0 else other),
                ).start()
    drain(dka.at[0], dk_recv.at[0])
    acc[...] = jnp.dot(xt[0], grad_rows(0, slice(None)), preferred_element_type=jnp.float32)
    drain(m_row, m_recv.at[0])
    m_y_out[...] = jnp.maximum(m_own[...], jnp.max(m_row[...], axis=0))
    for d in range(1, SIDE):
        remote(
            m_y_out, m_y_in.at[d - 1], m_send.at[1], m_recv.at[1], to(mate(1, d), f)
        ).start()
    drain(dka.at[1], dk_recv.at[1])

    own = pick(c, y, x)

    def slab_grad(target, cols):
        at = span(target * SLAB, SLAB)
        return acc[at, cols] + jnp.dot(
            xt[1, at], grad_rows(1, cols), preferred_element_type=jnp.float32
        )

    parts = [slice(p * PART, (p + 1) * PART) for p in range(COLS // PART)]
    for p, cols in enumerate(parts):
        for d in FAR_FIRST:
            y_out[p, d - 1] = slab_grad(lax.rem(own + d, SIDE), cols).astype(jnp.bfloat16)
            remote(
                y_out.at[p, d - 1], y_in.at[p, d - 1], y_send.at[p], y_recv.at[p],
                to(pick(c, mate(1, d), mate(0, d)), f),
            ).start()
    sums = [slab_grad(own, cols) for cols in parts]
    drain(m_y_in, m_recv.at[1])
    m_z_out[...] = jnp.maximum(m_y_out[...], jnp.max(m_y_in[...], axis=0))

    def last_sends(k, src, dst, send, recv):
        target = SIDE * c + k

        def away():
            remote(src, dst, send, recv, to(u, target)).start()

        def stay():
            pltpu.make_async_copy(src, dst, recv).start()

        pl.when(target != f)(away)
        pl.when(target == f)(stay)

    for k in range(SIDE):
        last_sends(k, m_z_out, m_z_in.at[z], m_send.at[2], m_recv.at[2])
    for p in range(len(parts)):
        drain(y_in.at[p], y_recv.at[p])
        for d in range(SIDE - 1):
            sums[p] += y_in[p, d].astype(jnp.float32)
        z_out[p] = sums[p].reshape(SIDE, OUT_ROWS, PART).astype(jnp.bfloat16)
        for k in range(SIDE):
            last_sends(k, z_out.at[p, k], z_in.at[p, z], z_send.at[p], z_recv.at[p])
    drain(m_z_in, m_recv.at[2])
    largest = jnp.max(m_z_in[...], axis=0)
    input_top = jnp.max(largest[0:4], axis=0, keepdims=True)[:, 0:1]
    key_top = jnp.max(largest[4:8], axis=0, keepdims=True)[:, 0:1]
    factor = 36.0 / (input_top * key_top) / math.sqrt(SEQ * FSDP * ULY * TOK)
    for p, cols in enumerate(parts):
        drain(z_in.at[p], z_recv.at[p])
        raw = z_in[p, 0].astype(jnp.float32)
        for source_z in range(1, SIDE):
            raw += z_in[p, source_z].astype(jnp.float32)
        out_ref[:, cols] = (raw * factor).astype(jnp.bfloat16)

    for s in range(SEQ):
        drain(kv.at[:, s, 0, 0:SIDE - 1], kv_send.at[s])

        def drain_same(s=s):
            drain(part_in.at[s], dk_send.at[s, 0])
            drain(part.at[s], dk_send.at[s, 1])

        def drain_other(s=s):
            drain(part.at[s], dk_send.at[s, 0])
            drain(xt.at[s, 0:(ULY - 1) * TOK * HD // (2 * SIDE * TOK)], dk_send.at[s, 1])

        pl.when(c == s)(drain_same)
        pl.when(c != s)(drain_other)
    drain(qg.at[1, 0:SIDE - 1], q_send.at[1])
    kv_left(1)
    drain(part_in.at[0], part_send)
    drain(qg.at[0, 0:SIDE - 1], q_send.at[0])
    kv_left(0)
    for n in range(SIDE):
        drain(part_in.at[1, 0:SIDE - 1, n], chunk_send.at[n])
    drain(xr.at[:, 0, 0:SIDE - 1], x_send.at[0])
    drain(xr.at[:, 1], x_send.at[1])
    for p in range(len(parts)):
        drain(y_in.at[p], y_send.at[p])
    drain(m_row, m_send.at[0])
    drain(m_y_in, m_send.at[1])

    def drain_last(count):
        for p in range(len(parts)):
            drain(z_in.at[p, 0:count], z_send.at[p])
        drain(m_z_in.at[0:count], m_send.at[2])

    pl.when(home == c)(lambda: drain_last(SIDE - 1))
    pl.when(home != c)(lambda: drain_last(SIDE))


def per_device(inputs_norm, queries, key_states, value_states, context_grad):
    bf16, f32 = jnp.bfloat16, jnp.float32
    parts = COLS // PART
    vmem, dma = pltpu.VMEM, pltpu.SemaphoreType.DMA
    return pl.pallas_call(
        kernel,
        out_shape=jax.ShapeDtypeStruct((OUT_ROWS, COLS), bf16),
        in_specs=[pl.BlockSpec(memory_space=pl.ANY)] * 5,
        out_specs=pl.BlockSpec(memory_space=pltpu.VMEM),
        scratch_shapes=[
            vmem((SEQ, SIDE, 2, TOK, GROUP * HD), bf16),
            vmem((2, SEQ, SIDE, SIDE, TOK, HD), bf16),
            vmem((SEQ, 2, SIDE, TOK, BAND), bf16),
            vmem((SEQ, BAND, 2 * SIDE * TOK), bf16),
            vmem((SEQ, SIDE, SIDE, TOK, HD), f32),
            vmem((SEQ, SIDE, SIDE, TOK, HD), bf16),
            vmem((SEQ, SIDE - 1, SIDE, TOK, HD), bf16),
            vmem((SEQ, SIDE, TOK, HD), bf16),
            vmem((SEQ, 2, SIDE, TOK, COLS), bf16),
            vmem((BAND, COLS), f32),
            vmem((parts, SIDE - 1, SLAB, PART), bf16),
            vmem((parts, SIDE - 1, SLAB, PART), bf16),
            vmem((parts, SIDE, OUT_ROWS, PART), bf16),
            vmem((parts, SIDE, OUT_ROWS, PART), bf16),
            vmem((8, HD), f32),
            vmem((8, HD), f32),
            vmem((2 * SIDE - 1, 8, HD), f32),
            vmem((8, HD), f32),
            vmem((SIDE - 1, 8, HD), f32),
            vmem((8, HD), f32),
            vmem((SIDE, 8, HD), f32),
            dma((SEQ, SIDE)), dma((SEQ,)), dma((SEQ, SIDE)), dma, dma, dma((SIDE,)),
            dma((SEQ,)), dma((parts,)), dma((parts,)), dma((3,)),
            dma((SEQ,)), dma((SEQ,)), dma((SEQ, SIDE)), dma((2,)), dma, dma((SIDE,)),
            dma((SEQ, 2)), dma((parts,)), dma((parts,)), dma((3,)),
        ],
        compiler_params=pltpu.CompilerParams(
            collective_id=0, has_side_effects=True, vmem_limit_bytes=56 * 1024 * 1024
        ),
    )(inputs_norm, queries, key_states, value_states, context_grad)


def solution(mesh):
    placed = P(("rep", "fsdp"), "uly", None)
    return jax.shard_map(
        per_device,
        mesh=mesh,
        in_specs=(placed,) * 5,
        out_specs=P(("rep", "uly", "fsdp"), None),
        check_vma=False,
    )
```
